256 devices in a mesh: dp: 8 (over y, core), expert: 32 (over z, x).
Axes of the slice: x: 4, y: 4, z: 8, core: 2. Of those that a mesh axis runs over, the one named last changes fastest.
Arguments:
- tokens: bfloat16 [32768, 2048], P(('dp', 'expert')), may hold values from -6 to 6
- cotangent: bfloat16 [32768, 2048], P(('dp', 'expert')), may hold values from -1.5 to 1.5
- routes: int32 [32768, 1], P(('dp', 'expert')), may hold values from 0 to 31; in each aligned block of 128 rows (0 to 127, 128 to 255, ...) at most 5 rows name the same one
- gates: bfloat16 [32768, 1], P(('dp', 'expert')), may hold values from 0.049804688 to 0.59765625
- loss_mask: int32 [32768], P(('dp', 'expert')), may hold values 0 or 1
- w_gate: bfloat16 [32, 1536, 2048], P('expert', 'dp'), may hold values from -0.125 to 0.125
- w_up: bfloat16 [32, 1536, 2048], P('expert', 'dp'), may hold values from -0.125 to 0.125
- w_down: bfloat16 [32, 1536, 2048], P('expert', 'dp'), may hold values from -0.15625 to 0.15625
Outputs:
- grad_tokens: bfloat16 [32768, 2048], P(('dp', 'expert'))
- grad_gates: float32 [32768, 1], P(('dp', 'expert'))
- grad_w_gate: bfloat16 [32, 1536, 2048], P('expert', 'dp')
- grad_w_up: bfloat16 [32, 1536, 2048], P('expert', 'dp')
- grad_w_down: bfloat16 [32, 1536, 2048], P('expert', 'dp')
The draws below stay inside these ranges and needn't reach their ends.
Inputs may be any that keep to these rules, and one draw needn't show every extreme that they name: `routes`: each row names 1 expert. Within the 128 rows of one device, no expert is named by more than 5 rows, a bound that some block reaches.
All inputs are finite; a program needn't handle non-finite values. No bound on the sum of `loss_mask` on one device may be relied on, other than what follows from the above.
Results may differ from the reference program's by a relative error of at most 0.02.
Values may be sent and summed in bfloat16 or wider, within the bound.
No kernel may reach another device: no remote copies, remote signals or barrier semaphores. Data moves between devices by JAX's collectives and lax.ppermute only.
A program may use at most 128 MiB of HBM per device.

```python
import math
import jax
import jax.numpy as jnp
import numpy as np
from jax import lax

D = 2048
FF = 1536
TOPK = 1
TOK_DEV = 128
EXPERTS = 32
CAP = 5
TOKENS = 32768
N_DP = 8
N_EXPERT = 32


def set_ends(result, rng, least, largest):
    index_at = [jax.random.randint(jax.random.fold_in(rng, axis), (), 0, length) for axis, length in enumerate(result.shape)]
    longest = result.shape.index(max(result.shape))
    beside = index_at[:longest] + [(index_at[longest] + 1) % result.shape[longest]] + index_at[longest + 1:]
    return result.at[tuple(index_at)].set(least).at[tuple(beside)].set(largest)


def block_scale(key, dims, cuts, smallest, top_value):
    def one(axis_at, parts):
        steps = jax.random.uniform(jax.random.fold_in(jax.random.fold_in(key, 6), axis_at), (parts,), jnp.float32, smallest / len(cuts), top_value / len(cuts))
        return jnp.repeat(jnp.exp(steps), dims[axis_at] // parts).reshape((-1,) + (1,) * (len(dims) - axis_at - 1))

    gain = one(*cuts[0])
    for cut in cuts[1:]:
        gain = gain * one(*cut)
    return gain


def routed_block(own_key, own, number, rows, count, top, reach, slope):
    ranking = jax.random.permutation(own_key, count)
    crowded, ordinary = shares(count, rows * top, reach, slope, True), shares(count, rows * top, reach, slope, False)
    places = jnp.arange(count)

    def named(lengths, turn):
        used = int((lengths > 0).sum())
        fixed = max(1, used // 4)
        shifted = fixed + (places - fixed + turn * (used - fixed)) % max(1, count - fixed)
        return jnp.zeros((count,), jnp.int32).at[ranking[jnp.where(places < fixed, places, shifted)]].set(jnp.asarray(lengths, jnp.int32))

    lengths = jnp.where(number % 4 == 0, named(crowded, number // 4), named(ordinary, number - number // 4 - 1))
    mixed = jax.random.permutation(jax.random.fold_in(own, 3), count)
    giver, sink = mixed[0:count // 2 * 2:2], mixed[1:count // 2 * 2:2]
    room = jnp.minimum(lengths[giver] - 1, reach - lengths[sink]) // 2
    room = jnp.where((giver == ranking[0]) | (sink == ranking[0]) | (lengths[sink] == 0), 0, jnp.maximum(room, 0))
    shifted = jax.random.randint(jax.random.fold_in(own, 4), (count // 2,), 0, 1 << 20) % (room + 1)
    lengths = lengths.at[giver].add(-shifted).at[sink].add(shifted)
    items = jnp.searchsorted(jnp.cumsum(lengths), jnp.arange(rows * top), side="right").astype(jnp.int32)
    listing = items.reshape(top, rows).T
    listing = listing[jax.random.permutation(jax.random.fold_in(own, 1), rows)]
    turn = jax.random.randint(jax.random.fold_in(own, 2), (rows, 1), 0, top)
    return jnp.take_along_axis(listing, (jnp.arange(top)[None, :] + turn) % top, axis=1)


def shares(count, total, reach, lean, full):
    weights = [(1 << 20) // math.isqrt(rank ** lean) + 1 for rank in range(1, count + 1)]
    largest = reach if full else min(reach, max(-(-total // count), total * weights[0] // sum(weights)))
    least = 1 if total - largest >= count - 1 else 0
    counts, surplus = [largest] + [least] * (count - 1), total - largest - least * (count - 1)
    while surplus > 0:
        candidates = [i for i in range(1, count) if counts[i] < largest] or [i for i in range(1, count) if counts[i] < reach]
        pool, left = sum([weights[i] for i in candidates]), surplus
        for i in candidates:
            extra = min(reach - counts[i], max(1, left * weights[i] // pool), surplus)
            counts[i] = counts[i] + extra
            surplus = surplus - extra
    return np.array(counts)


def scatter_about(own_key, extent, deviation, limit, shards=(), held_as=jnp.bfloat16):
    drawn = deviation * jax.random.normal(own_key, extent, jnp.float32)
    if shards:
        drawn = drawn * block_scale(own_key, extent, shards, -0.22, 0.18)
    return jnp.clip(drawn, -limit, limit).astype(held_as)


def setup_inputs(seed: int = 0) -> dict:
    key_of = jax.random.split(jax.random.key(seed), 9)
    tokens = scatter_about(key_of[0], (TOKENS, D), 1.0, 6.0, ((0, 256),))
    cotangent = scatter_about(key_of[1], (TOKENS, D), 0.25, 1.5, ((0, 256),))
    routes_keys = jax.random.split(jax.random.fold_in(key_of[2], 1), TOKENS // TOK_DEV)
    routes_turns = jax.random.permutation(jax.random.fold_in(key_of[2], 3), TOKENS // TOK_DEV)
    routes = jax.vmap(lambda own, number: routed_block(jax.random.fold_in(key_of[2], 2), own, number, TOK_DEV, EXPERTS, TOPK, CAP, 2))(routes_keys, routes_turns).reshape((TOKENS, TOPK))
    gates = jnp.clip(0.049804688 + 0.54785156 * jax.random.uniform(key_of[3], (TOKENS, TOPK), jnp.float32) ** block_scale(key_of[3], (TOKENS, TOPK), ((0, 256),), -0.2, 0.2), 0.049804688, 0.59765625).astype(jnp.bfloat16)
    loss_mask = set_ends((jax.random.randint(key_of[4], (TOKENS,), 0, 4) < 3).astype(jnp.int32), jax.random.fold_in(key_of[4], 1), 0, 1)
    w_gate = scatter_about(key_of[5], (EXPERTS, FF, D), D ** -0.5, 0.125, ((0, 32), (1, 8)))
    w_up = scatter_about(key_of[6], (EXPERTS, FF, D), D ** -0.5, 0.125, ((0, 32), (1, 8)))
    w_down = scatter_about(key_of[7], (EXPERTS, FF, D), FF ** -0.5, 0.15625, ((0, 32), (1, 8)))
    return dict(tokens=tokens, cotangent=cotangent, routes=routes, gates=gates, loss_mask=loss_mask, w_gate=w_gate, w_up=w_up, w_down=w_down)


def reference(tokens, cotangent, routes, gates, loss_mask, w_gate, w_up, w_down):
    masked = jnp.where((loss_mask == 1)[:, None], cotangent, jnp.zeros_like(cotangent))
    row_count = N_DP * N_EXPERT * CAP
    part_count = N_DP
    part_width = FF // N_DP

    def expert_step(totals, expert_id):
        grad_rows, grad_slots = totals
        chosen = routes == expert_id
        present = jnp.any(chosen, axis=1)
        row_order = jnp.argsort(jnp.where(present, 0, 1).astype(jnp.int32), stable=True)[:row_count].astype(jnp.int32)
        live_rows = present[row_order]
        gate_rows = jnp.sum(jnp.where(chosen, gates.astype(jnp.float32), jnp.float32(0.0)), axis=1)[row_order]
        gate_rows = jnp.where(live_rows, gate_rows, jnp.float32(0.0))
        rows_x = tokens[row_order]
        rows_dy = jnp.where(live_rows[:, None], masked[row_order], jnp.zeros_like(masked[row_order]))
        gate_mat = w_gate[expert_id]
        up_mat = w_up[expert_id]
        down_mat = w_down[expert_id]
        pre_gate = jnp.dot(rows_x, gate_mat.T, preferred_element_type=jnp.float32)
        pre_up = jnp.dot(rows_x, up_mat.T, preferred_element_type=jnp.float32)
        back_proj = jnp.dot(rows_dy, down_mat.T, preferred_element_type=jnp.float32)
        sigmoid_gate = jax.nn.sigmoid(pre_gate)
        activated = pre_gate * sigmoid_gate
        hidden = (activated * pre_up).astype(jnp.bfloat16)
        d_hidden = gate_rows[:, None] * back_proj
        d_pre_gate = (d_hidden * pre_up * sigmoid_gate * (1.0 + pre_gate * (1.0 - sigmoid_gate))).astype(jnp.bfloat16)
        d_pre_up = (d_hidden * activated).astype(jnp.bfloat16)
        scaled_dy = (gate_rows[:, None] * rows_dy.astype(jnp.float32)).astype(jnp.bfloat16)
        grad_down = jnp.dot(hidden.T, scaled_dy, preferred_element_type=jnp.float32).astype(jnp.bfloat16)
        grad_gate = jnp.dot(d_pre_gate.T, rows_x, preferred_element_type=jnp.float32).astype(jnp.bfloat16)
        grad_up = jnp.dot(d_pre_up.T, rows_x, preferred_element_type=jnp.float32).astype(jnp.bfloat16)
        split_gate = d_pre_gate.astype(jnp.float32).reshape(row_count, part_count, part_width)
        split_up = d_pre_up.astype(jnp.float32).reshape(row_count, part_count, part_width)
        mats_gate = gate_mat.astype(jnp.float32).reshape(part_count, part_width, D)
        mats_up = up_mat.astype(jnp.float32).reshape(part_count, part_width, D)
        partial_rows = jnp.einsum("rqf,qfd->rqd", split_gate, mats_gate) + jnp.einsum("rqf,qfd->rqd", split_up, mats_up)
        partial_rows = lax.optimization_barrier(partial_rows.astype(jnp.bfloat16))
        row_sum = jnp.sum(partial_rows.astype(jnp.float32), axis=1)
        slot_part = jnp.sum((hidden.astype(jnp.float32) * back_proj).reshape(row_count, part_count, part_width), axis=2)
        slot_part = lax.optimization_barrier(slot_part.astype(jnp.bfloat16))
        slot_sum = jnp.sum(slot_part.astype(jnp.float32), axis=1)
        grad_rows = grad_rows.at[row_order].add(row_sum)
        token_slot = jnp.zeros((TOKENS,), jnp.float32).at[row_order].add(slot_sum)
        grad_slots = grad_slots + jnp.where(chosen, token_slot[:, None], jnp.float32(0.0))
        return (grad_rows, grad_slots), (grad_gate, grad_up, grad_down)

    start = (jnp.zeros((TOKENS, D), jnp.float32), jnp.zeros((TOKENS, TOPK), jnp.float32))
    (grad_rows, grad_slots), stacked = lax.scan(expert_step, start, jnp.arange(EXPERTS, dtype=jnp.int32))
    return grad_rows.astype(jnp.bfloat16), grad_slots, stacked[0], stacked[1], stacked[2]
```

```python
import functools
import math

import jax
import jax.numpy as jnp
from jax import lax
from jax.experimental import pallas as pl
from jax.experimental.pallas import tpu as pltpu
from jax.sharding import Mesh, PartitionSpec as P

SLOTS = 5
BF = jnp.bfloat16
F32 = jnp.float32
LIMIT = 56 * 1024 * 1024


def dot(a, b, dims=((1,), (0,))):
    return lax.dot_general(a, b, (dims, ((), ())), preferred_element_type=F32)


def iota(shape, axis):
    return lax.broadcasted_iota(jnp.int32, shape, axis)


def params():
    return pltpu.CompilerParams(vmem_limit_bytes=LIMIT)


def vmem(count):
    return [pl.BlockSpec(memory_space=pltpu.VMEM)] * count


def places(routes_row, experts):
    tokens = routes_row.shape[1]
    picked = iota((experts, tokens), 0) == routes_row
    hot = jnp.where(picked, 1.0, 0.0).astype(BF)
    earlier = jnp.where(iota((tokens, tokens), 0) < iota((tokens, tokens), 1), 1.0, 0.0).astype(BF)
    before = dot(hot, earlier)
    rank = jnp.sum(jnp.where(picked, before, 0.0), axis=0, keepdims=True).astype(jnp.int32)
    return routes_row, rank


def main_rows(expert, rank, half):
    return jnp.where(rank < SLOTS - 1, expert * 8 + half * 4 + rank, -1)


def last_rows(expert, rank, piece):
    return jnp.where(rank == SLOTS - 1, expert * 8 + piece, -1)


def one_hot(rows, target):
    return iota((rows, target.shape[1]), 0) == target


def pack_tokens(routes_ref, gates_ref, mask_ref, x_ref, dy_ref, px_ref, pdy_ref):
    width = x_ref.shape[1]
    rows = px_ref.shape[0]
    half, piece = width // 2, width // 8
    expert, rank = places(routes_ref[...], rows // 8)
    weight = jnp.where(mask_ref[...] == 1, gates_ref[...].astype(F32), 0.0)
    for src, dst, scale in ((x_ref, px_ref, None), (dy_ref, pdy_ref, weight)):
        def spread(target):
            value = 1.0 if scale is None else scale
            return jnp.where(one_hot(rows, target), value, 0.0).astype(BF)

        main = dot(spread(main_rows(expert, rank, 0)), src[:, :half])
        main += dot(spread(main_rows(expert, rank, 1)), src[:, half:])
        dst[:, :half] = main.astype(BF)
        last = jnp.zeros((rows, piece), F32)
        for k in range(8):
            last += dot(spread(last_rows(expert, rank, k)), src[:, k * piece : (k + 1) * piece])
        dst[:, half : half + piece] = last.astype(BF)


def unpack_tokens(routes_ref, gates_ref, r_ref, out_ref, gate_ref):
    width = out_ref.shape[1]
    rows = r_ref.shape[0]
    half, piece = width // 2, width // 8
    expert, rank = places(routes_ref[...], rows // 8)

    def spread(target):
        return jnp.where(one_hot(rows, target), 1.0, 0.0).astype(BF)

    across = ((0,), (0,))
    mains = [dot(spread(main_rows(expert, rank, h)), r_ref[:, :half], across) for h in (0, 1)]
    for k in range(8):
        last = dot(spread(last_rows(expert, rank, k)), r_ref[:, half : half + piece], across)
        at = (k % 4) * piece
        out_ref[:, k * piece : (k + 1) * piece] = (mains[k // 4][:, at : at + piece] + last).astype(BF)
    lanes = r_ref[:, half + piece :]
    summed = dot(lanes, spread(expert * 8 + rank), across)
    gate_ref[...] = summed[0:1, :] / gates_ref[...].astype(F32)


def main_order(rows):
    at = iota((rows, rows), 1)
    inner = at % (rows // 2)
    return iota((rows, rows), 0) == (inner // 4) * 8 + (at // (rows // 2)) * 4 + inner % 4


def last_order(rows):
    at = iota((rows, rows), 1)
    return iota((rows, rows), 0) == (at % (rows // 8)) * 8 + at // (rows // 8)


def expert_rows(xs, dys, weights, outs, x_ref, dy_ref, act_refs, wgu, wd, pre, back, dcat):
    rows = xs[0].shape[0]
    width = x_ref.shape[1]
    half, piece = width // 2, width // 8
    units = weights[0].shape[0]
    both = 2 * units
    four = rows // 2
    lone = rows // 8
    block = four + lone
    for i, (gate_w, up_w, down_w) in enumerate((weights[:3], weights[3:])):
        wgu[i * units : (i + 1) * units] = gate_w[...]
        wgu[both + i * units : both + (i + 1) * units] = up_w[...]
        wd[i * units : (i + 1) * units] = down_w[...]
    order = jnp.where(main_order(rows), 1.0, 0.0).astype(BF)
    order_last = jnp.where(last_order(rows), 1.0, 0.0).astype(BF)
    across = ((0,), (0,))
    lanes_of = ((1,), (1,))
    for parts, dst in ((xs, x_ref), (dys, dy_ref)):
        for b in range(4):
            if b < 3:
                got_main, got_last = parts[b][:, :half], parts[b][:, half : half + piece]
            else:
                got = jnp.concatenate([parts[3][...], parts[4][...]], axis=0)
                got_main, got_last = got[:, :half], got[:, half : half + piece]
            main = dot(order, got_main, across).astype(BF)
            last = dot(order_last, got_last, across).astype(BF)
            at = b * block
            dst[at : at + four, :half] = main[:four]
            dst[at : at + four, half:] = main[four:]
            for k in range(8):
                dst[at + four : at + block, k * piece : (k + 1) * piece] = last[k * lone : (k + 1) * lone]
    pre[...] = dot(x_ref[...], wgu[...], lanes_of)
    back[...] = dot(dy_ref[...], wd[...], lanes_of)
    hid_ref = act_refs[0]
    total = 4 * block
    step = math.gcd(block, 32)
    gates = []
    for r in range(0, total, step):
        at = slice(r, r + step)
        gate, up, bp = pre[at, :both], pre[at, both:], back[at, :]
        sig = jax.nn.sigmoid(gate)
        silu = gate * sig
        hidden = (silu * up).astype(BF)
        hid_ref[at, :] = hidden
        dcat[at, :both] = (bp * up * sig * (1.0 + gate * (1.0 - sig))).astype(BF)
        dcat[at, both:] = (bp * silu).astype(BF)
        gates.append(jnp.sum(hidden.astype(F32) * bp, axis=1, keepdims=True))
    act_refs[1][...] = dcat[...]
    for b in range(4):
        at = b * block
        part = dot(dcat[at : at + block, :], wgu[...]).astype(BF)
        stacked = jnp.concatenate([part[:four, :half], part[:four, half:]], axis=0)
        outs[b][:, :half] = dot(order, stacked).astype(BF)
        stacked = jnp.concatenate([part[four:, k * piece : (k + 1) * piece] for k in range(8)], axis=0)
        outs[b][:, half : half + piece] = dot(order_last, stacked).astype(BF)
        column = jnp.concatenate(gates[at // step : (at + block) // step], axis=0)
        column = jnp.broadcast_to(column.astype(BF), (block, 128))
        main = dot(order[:, :four], column[:four])
        pick = iota((rows, lone), 0) == iota((rows, lone), 1) * 8 + 4
        main += dot(jnp.where(pick, 1.0, 0.0).astype(BF), column[four:])
        outs[b][:, half + piece :] = main.astype(BF)


def call_expert_rows(xs, dys, weights):
    rows, packed = xs[0].shape
    units, width = weights[0].shape
    total = 4 * (rows // 2 + rows // 8)

    def body(*refs):
        ins, rest = refs[:16], refs[16:]
        outs, rest = rest[:8], rest[8:]
        expert_rows(ins[:5], ins[5:10], ins[10:16], outs[:4], outs[4], outs[5], outs[6:8], *rest)

    return pl.pallas_call(
        body,
        out_shape=[jax.ShapeDtypeStruct((rows, packed + 128), BF)] * 4
        + [jax.ShapeDtypeStruct((total, width), BF)] * 2
        + [jax.ShapeDtypeStruct((total, 2 * units), BF), jax.ShapeDtypeStruct((total, 4 * units), BF)],
        in_specs=vmem(16),
        out_specs=vmem(8),
        scratch_shapes=[
            pltpu.VMEM((4 * units, width), BF),
            pltpu.VMEM((2 * units, width), BF),
            pltpu.VMEM((total, 4 * units), F32),
            pltpu.VMEM((total, 2 * units), F32),
            pltpu.VMEM((total, 4 * units), BF),
        ],
        compiler_params=params(),
        cost_estimate=pl.CostEstimate(
            flops=10 * 2 * total * units * width, bytes_accessed=24 * total * width, transcendentals=total * 2 * units
        ),
    )(*xs, *dys, *weights)


def grad_block(own, has_more, units, *refs):
    hid_ref, d_ref, x_ref, dy_ref = refs[:4]
    more = refs[4 : 4 + 3 * has_more]
    outs = refs[4 + 3 * has_more :]
    both = 2 * units
    first = 0 if own else units
    across = ((0,), (0,))
    down = dot(hid_ref[...], dy_ref[...], across)[first : first + units]
    pair = dot(d_ref[...], x_ref[...], across)
    gate = pair[first : first + units]
    up = pair[both + first : both + first + units]
    for i, value in enumerate((gate, up, down)):
        if has_more:
            value = value + more[i][...].astype(F32)
        outs[i][...] = value.astype(BF)


def call_grads(own, hid, d, x, dy, more):
    total, width = x.shape
    units = hid.shape[1] // 2
    cols = 512
    full = lambda a: pl.BlockSpec(a.shape, lambda j: (0, 0))
    piece = lambda rows: pl.BlockSpec((rows, cols), lambda j: (0, j))
    return pl.pallas_call(
        functools.partial(grad_block, own, bool(more), units),
        grid=(width // cols,),
        out_shape=[jax.ShapeDtypeStruct((units, width), BF)] * 3,
        in_specs=[full(hid), full(d), piece(total), piece(total)] + [piece(units)] * len(more),
        out_specs=[piece(units)] * 3,
        compiler_params=params(),
        cost_estimate=pl.CostEstimate(
            flops=6 * 2 * total * units * width, bytes_accessed=4 * total * width + 12 * units * width, transcendentals=0
        ),
    )(hid, d, x, dy, *more)


def along(v, axis, size, by):
    return lax.ppermute(v, axis, [(i, (i + by) % size) for i in range(size)])


def shards(tokens, cotangent, routes, gates, loss_mask, w_gate, w_up, w_down):
    experts = lax.axis_size("z") * lax.axis_size("x")
    ring = lax.axis_size("y")
    count, width = tokens.shape
    packed = width // 2 + width // 8
    rows = experts * 8
    flip = lambda v: along(v, "core", 2, 1)
    mine = [w_gate[0], w_up[0], w_down[0]]
    theirs = [flip(w) for w in mine]
    routes_row = routes.reshape(1, count)
    gates_row = gates.reshape(1, count)
    mask_row = loss_mask.reshape(1, count)
    px, pdy = pl.pallas_call(
        pack_tokens,
        out_shape=[jax.ShapeDtypeStruct((rows, packed), BF)] * 2,
        in_specs=vmem(5),
        out_specs=vmem(2),
        compiler_params=params(),
    )(routes_row, gates_row, mask_row, tokens, cotangent)

    def dispatch(v):
        chunks = v.reshape(experts, 8, v.shape[1])
        return lax.all_to_all(chunks, ("z", "x"), 0, 0, tiled=True).reshape(v.shape)

    def gather(v):
        low, high = along(v, "y", ring, 1), along(v, "y", ring, -1)
        cut = rows // 2
        return [v, low, high, along(low[:cut], "y", ring, 1), along(high[cut:], "y", ring, -1)]

    xs = gather(dispatch(px))
    dys = gather(dispatch(pdy))
    *parts, x_all, dy_all, hid, d = call_expert_rows(xs, dys, mine + theirs)
    home = parts[0].astype(F32)
    for part, by in zip(parts[1:], (-1, 1, 2)):
        home = home + along(part, "y", ring, by).astype(F32)
    given = call_grads(False, hid, d, x_all, dy_all, [])
    taken = [flip(g) for g in given]
    returned = dispatch(home.astype(BF))
    grads = call_grads(True, hid, d, x_all, dy_all, taken)
    grad_tokens, grad_gates = pl.pallas_call(
        unpack_tokens,
        out_shape=[jax.ShapeDtypeStruct((count, width), BF), jax.ShapeDtypeStruct((1, count), F32)],
        in_specs=vmem(3),
        out_specs=vmem(2),
        compiler_params=params(),
    )(routes_row, gates_row, returned)
    return (grad_tokens, grad_gates.reshape(count, 1), *[g[None] for g in grads])


def solution(mesh):
    devices = mesh.devices
    fine = Mesh(devices.reshape(devices.shape[0] // 2, 2, -1, 4), ("y", "core", "z", "x"))
    row = P(("y", "core", "z", "x"))
    weight = P(("z", "x"), ("y", "core"))
    return jax.shard_map(
        shards,
        mesh=fine,
        in_specs=(row,) * 5 + (weight,) * 3,
        out_specs=(row,) * 2 + (weight,) * 3,
        check_vma=False,
    )
```

```python
import functools
import math

import jax
import jax.numpy as jnp
from jax import lax
from jax.experimental import pallas as pl
from jax.experimental.pallas import tpu as pltpu
from jax.sharding import Mesh, PartitionSpec as P

SLOTS = 5
BF = jnp.bfloat16
F32 = jnp.float32
ACROSS = ((0,), (0,))
LANES = ((1,), (1,))


def dot(a, b, dims=((1,), (0,))):
    return lax.dot_general(a, b, (dims, ((), ())), preferred_element_type=F32)


def iota(shape, axis):
    return lax.broadcasted_iota(jnp.int32, shape, axis)


def params(size=24):
    return pltpu.CompilerParams(vmem_limit_bytes=size * 1024 * 1024)


def vmem(count):
    return [pl.BlockSpec(memory_space=pltpu.VMEM)] * count


def places(routes_row, experts):
    tokens = routes_row.shape[1]
    picked = iota((experts, tokens), 0) == routes_row
    hot = jnp.where(picked, 1.0, 0.0).astype(BF)
    earlier = jnp.where(iota((tokens, tokens), 0) < iota((tokens, tokens), 1), 1.0, 0.0).astype(BF)
    before = dot(hot, earlier)
    rank = jnp.sum(jnp.where(picked, before, 0.0), axis=0, keepdims=True).astype(jnp.int32)
    return routes_row, rank


def main_rows(expert, rank, half):
    return jnp.where(rank < SLOTS - 1, expert * 8 + half * 4 + rank, -1)


def last_rows(expert, rank, piece):
    return jnp.where(rank == SLOTS - 1, expert * 8 + piece, -1)


def one_hot(rows, target):
    return iota((rows, target.shape[1]), 0) == target


def pack_tokens(scaled, *refs):
    if scaled:
        routes_ref, gates_ref, mask_ref, src, dst = refs
        value = jnp.where(mask_ref[...] == 1, gates_ref[...].astype(F32), 0.0)
    else:
        routes_ref, src, dst = refs
        value = 1.0
    width = src.shape[1]
    rows = dst.shape[0]
    half, piece = width // 2, width // 8
    expert, rank = places(routes_ref[...], rows // 8)

    def spread(target):
        return jnp.where(one_hot(rows, target), value, 0.0).astype(BF)

    main = dot(spread(main_rows(expert, rank, 0)), src[:, :half])
    main += dot(spread(main_rows(expert, rank, 1)), src[:, half:])
    dst[:, :half] = main.astype(BF)
    last = jnp.zeros((rows, piece), F32)
    for k in range(8):
        last += dot(spread(last_rows(expert, rank, k)), src[:, k * piece : (k + 1) * piece])
    dst[:, half:] = last.astype(BF)


def unpack_tokens(routes_ref, gates_ref, r_ref, out_ref, gate_ref):
    width = out_ref.shape[1]
    rows = r_ref.shape[0]
    half, piece = width // 2, width // 8
    expert, rank = places(routes_ref[...], rows // 8)

    def spread(target):
        return jnp.where(one_hot(rows, target), 1.0, 0.0).astype(BF)

    mains = [dot(spread(main_rows(expert, rank, h)), r_ref[:, :half], ACROSS) for h in (0, 1)]
    for k in range(8):
        last = dot(spread(last_rows(expert, rank, k)), r_ref[:, half : half + piece], ACROSS)
        at = (k % 4) * piece
        out_ref[:, k * piece : (k + 1) * piece] = (mains[k // 4][:, at : at + piece] + last).astype(BF)
    lanes = r_ref[:, half + piece :]
    summed = dot(lanes, spread(expert * 8 + rank), ACROSS)
    gate_ref[...] = summed[0:1, :] / gates_ref[...].astype(F32)


def main_order(rows):
    at = iota((rows, rows), 1)
    inner = at % (rows // 2)
    return iota((rows, rows), 0) == (inner // 4) * 8 + (at // (rows // 2)) * 4 + inner % 4


def last_order(rows):
    at = iota((rows, rows), 1)
    return iota((rows, rows), 0) == (at % (rows // 8)) * 8 + at // (rows // 8)


def orders(rows):
    order = jnp.where(main_order(rows), 1.0, 0.0).astype(BF)
    return order, jnp.where(last_order(rows), 1.0, 0.0).astype(BF)


def open_chunks(packed, dst, at, order, order_last):
    rows = packed.shape[0]
    width = dst.shape[1]
    half, piece = width // 2, width // 8
    four, lone = rows // 2, rows // 8
    main = dot(order, packed[:, :half], ACROSS).astype(BF)
    last = dot(order_last, packed[:, half:], ACROSS).astype(BF)
    dst[at : at + four, :half] = main[:four]
    dst[at : at + four, half:] = main[four:]
    for k in range(8):
        dst[at + four : at + four + lone, k * piece : (k + 1) * piece] = last[k * lone : (k + 1) * lone]


def close_chunks(part, column, out, order, order_last):
    rows = out.shape[0]
    width = part.shape[1]
    half, piece = width // 2, width // 8
    four, lone = rows // 2, rows // 8
    stacked = jnp.concatenate([part[:four, :half], part[:four, half:]], axis=0)
    out[:, :half] = dot(order, stacked).astype(BF)
    stacked = jnp.concatenate([part[four:, k * piece : (k + 1) * piece] for k in range(8)], axis=0)
    out[:, half : half + piece] = dot(order_last, stacked).astype(BF)
    column = jnp.broadcast_to(column.astype(BF), (four + lone, 128))
    main = dot(order[:, :four], column[:four])
    pick = iota((rows, lone), 0) == iota((rows, lone), 1) * 8 + 4
    main += dot(jnp.where(pick, 1.0, 0.0).astype(BF), column[four:])
    out[:, half + piece :] = main.astype(BF)


def x_part(*refs):
    xs, wgu = refs[:4], refs[4]
    x_ref, hid_ref, slope_ref, silu_ref, pre = refs[5:]
    order, order_last = orders(xs[0].shape[0])
    total, both = hid_ref.shape
    block = total // 4
    for b in range(4):
        open_chunks(xs[b][...], x_ref, b * block, order, order_last)
    pre[...] = dot(x_ref[...], wgu[...], LANES)
    step = math.gcd(block, 32)
    for r in range(0, total, step):
        at = slice(r, r + step)
        gate, up = pre[at, :both], pre[at, both:]
        sig = jax.nn.sigmoid(gate)
        silu = gate * sig
        hid_ref[at, :] = (silu * up).astype(BF)
        slope_ref[at, :] = up * sig * (1.0 + gate * (1.0 - sig))
        silu_ref[at, :] = silu


def call_x_part(xs, wgu):
    rows, packed = xs[0].shape
    pairs, width = wgu.shape
    total = 4 * (rows // 2 + rows // 8)
    half_units = jax.ShapeDtypeStruct((total, pairs // 2), F32)
    return pl.pallas_call(
        x_part,
        out_shape=[
            jax.ShapeDtypeStruct((total, width), BF),
            jax.ShapeDtypeStruct((total, pairs // 2), BF),
            half_units,
            half_units,
        ],
        in_specs=vmem(5),
        out_specs=vmem(4),
        scratch_shapes=[pltpu.VMEM((total, pairs), F32)],
        compiler_params=params(),
        cost_estimate=pl.CostEstimate(
            flops=3 * total * pairs * width, bytes_accessed=4 * total * width, transcendentals=total * pairs // 2
        ),
    )(*xs, wgu)


def dy_part(first, blocks, ins, *refs):
    dys, (hid, slope, silu, wgu, wd) = refs[:ins], refs[ins : ins + 5]
    outs = refs[ins + 5 : ins + 5 + blocks]
    dy_ref, d_ref, back = refs[ins + 5 + blocks :]
    total = dy_ref.shape[0]
    both = wd.shape[0]
    block = total // blocks
    begin = first * block
    order, order_last = orders(outs[0].shape[0])
    for b in range(blocks):
        if ins > blocks:
            packed = jnp.concatenate([ref[...] for ref in dys], axis=0)
        else:
            packed = dys[b][...]
        open_chunks(packed, dy_ref, b * block, order, order_last)
    back[...] = dot(dy_ref[...], wd[...], LANES)
    step = math.gcd(block, 32)
    columns = []
    for r in range(0, total, step):
        at = slice(r, r + step)
        there = slice(begin + r, begin + r + step)
        bp = back[at, :]
        d_ref[at, :both] = (bp * slope[there, :]).astype(BF)
        d_ref[at, both:] = (bp * silu[there, :]).astype(BF)
        columns.append(jnp.sum(hid[there, :].astype(F32) * bp, axis=1, keepdims=True))
    for b in range(blocks):
        at = b * block
        part = dot(d_ref[at : at + block, :], wgu[...]).astype(BF)
        column = jnp.concatenate(columns[at // step : (at + block) // step], axis=0)
        close_chunks(part, column, outs[b], order, order_last)


def call_dy_part(first, blocks, dys, hid, slope, silu, wgu, wd):
    packed = dys[0].shape[1]
    both, width = wd.shape
    total = hid.shape[0] // 4 * blocks
    rows = hid.shape[0] // 4 * 8 // 5
    return pl.pallas_call(
        functools.partial(dy_part, first, blocks, len(dys)),
        out_shape=[jax.ShapeDtypeStruct((rows, packed + 128), BF)] * blocks
        + [jax.ShapeDtypeStruct((total, width), BF), jax.ShapeDtypeStruct((total, 2 * both), BF)],
        in_specs=vmem(len(dys) + 5),
        out_specs=vmem(blocks + 2),
        scratch_shapes=[pltpu.VMEM((total, both), F32)],
        compiler_params=params(),
        cost_estimate=pl.CostEstimate(
            flops=9 * total * both * width, bytes_accessed=6 * total * width, transcendentals=0
        ),
    )(*dys, hid, slope, silu, wgu, wd)


def grad_block(own, has_more, units, hid, d1, d2, x, dy1, dy2, *refs):
    out = refs[-1]
    cut = d1.shape[0]
    both = 2 * units
    first = 0 if own else units
    down = dot(hid[:cut], dy1[...], ACROSS) + dot(hid[cut:], dy2[...], ACROSS)
    pair = dot(d1[...], x[:cut], ACROSS) + dot(d2[...], x[cut:], ACROSS)
    values = (pair[first : first + units], pair[both + first : both + first + units], down[first : first + units])
    for i, value in enumerate(values):
        if has_more:
            refs[1 + i][...] = (value + refs[0][i * units : (i + 1) * units].astype(F32)).astype(BF)
        else:
            out[i * units : (i + 1) * units] = value.astype(BF)


def call_grads(own, hid, d1, d2, x, dy1, dy2, more):
    total, width = x.shape
    units = hid.shape[1] // 2
    cols = 512
    full = lambda a: pl.BlockSpec(a.shape, lambda j: (0, 0))
    piece = lambda rows: pl.BlockSpec((rows, cols), lambda j: (0, j))
    if more:
        out_shape, out_specs = [jax.ShapeDtypeStruct((units, width), BF)] * 3, [piece(units)] * 3
    else:
        out_shape, out_specs = [jax.ShapeDtypeStruct((3 * units, width), BF)], [piece(3 * units)]
    return pl.pallas_call(
        functools.partial(grad_block, own, bool(more), units),
        grid=(width // cols,),
        out_shape=out_shape,
        in_specs=[full(hid), full(d1), full(d2), piece(total), piece(dy1.shape[0]), piece(dy2.shape[0])]
        + [piece(3 * units)] * len(more),
        out_specs=out_specs,
        compiler_params=params(),
        cost_estimate=pl.CostEstimate(
            flops=12 * total * units * width, bytes_accessed=4 * total * width + 12 * units * width, transcendentals=0
        ),
    )(hid, d1, d2, x, dy1, dy2, *more)


def along(v, axis, size, by):
    return lax.ppermute(v, axis, [(i, (i + by) % size) for i in range(size)])


def shards(tokens, cotangent, routes, gates, loss_mask, w_gate, w_up, w_down):
    experts = lax.axis_size("z") * lax.axis_size("x")
    ring = lax.axis_size("y")
    count, width = tokens.shape
    packed = width // 2 + width // 8
    rows = experts * 8
    units = w_gate.shape[1]
    flip = lambda v: along(v, "core", 2, 1)
    mine = [w_gate[0], w_up[0], w_down[0]]
    swapped = flip(jnp.concatenate(mine, axis=0))
    theirs = [swapped[i * units : (i + 1) * units] for i in range(3)]
    wgu = jnp.concatenate([mine[0], theirs[0], mine[1], theirs[1]], axis=0)
    wd = jnp.concatenate([mine[2], theirs[2]], axis=0)
    routes_row = routes.reshape(1, count)
    gates_row = gates.reshape(1, count)
    mask_row = loss_mask.reshape(1, count)

    def pack(*operands):
        return pl.pallas_call(
            functools.partial(pack_tokens, len(operands) > 2),
            out_shape=jax.ShapeDtypeStruct((rows, packed), BF),
            in_specs=vmem(len(operands)),
            out_specs=vmem(1)[0],
            compiler_params=params(56),
        )(*operands)

    def dispatch(v):
        chunks = v.reshape(experts, 8, v.shape[1])
        return lax.all_to_all(chunks, ("z", "x"), 0, 0, tiled=True).reshape(v.shape)

    step = lambda v, by: along(v, "y", ring, by)
    x_own = dispatch(pack(routes_row, tokens))
    packed_dy = pack(routes_row, gates_row, mask_row, cotangent)
    x_own, packed_dy = lax.optimization_barrier((x_own, packed_dy))
    dy_own = dispatch(packed_dy)
    cut = rows // 2
    x_low, x_high = step(x_own, 1), step(x_own, -1)
    far = [step(x_low[:cut], 1), step(x_high[cut:], -1)]
    xs = [x_own, x_low, x_high, jnp.concatenate(far, axis=0)]
    x_all, hid, slope, silu = call_x_part(xs, wgu)
    low, high = step(dy_own, 1), step(dy_own, -1)
    far = [step(low[:cut], 1), step(high[cut:], -1)]
    p_own, p_low, p_high, dy1, d1 = call_dy_part(0, 3, [dy_own, low, high], hid, slope, silu, wgu, wd)
    p_far, dy2, d2 = call_dy_part(3, 1, far, hid, slope, silu, wgu, wd)
    arrived = [step(p_low, -1), step(p_high, 1), step(p_far, 2)]
    (given,) = call_grads(False, hid, d1, d2, x_all, dy1, dy2, [])
    *arrived, given = lax.optimization_barrier((*arrived, given))
    taken = flip(given)
    home = p_own.astype(F32)
    for part in arrived:
        home = home + part.astype(F32)
    returned = dispatch(home.astype(BF))
    grads = call_grads(True, hid, d1, d2, x_all, dy1, dy2, [taken])
    returned, *grads = lax.optimization_barrier((returned, *grads))
    grad_tokens, grad_gates = pl.pallas_call(
        unpack_tokens,
        out_shape=[jax.ShapeDtypeStruct((count, width), BF), jax.ShapeDtypeStruct((1, count), F32)],
        in_specs=vmem(3),
        out_specs=vmem(2),
        compiler_params=params(),
    )(routes_row, gates_row, returned)
    return (grad_tokens, grad_gates.reshape(count, 1), *[g[None] for g in grads])


def solution(mesh):
    devices = mesh.devices
    fine = Mesh(devices.reshape(devices.shape[0] // 2, 2, -1, 4), ("y", "core", "z", "x"))
    row = P(("y", "core", "z", "x"))
    weight = P(("z", "x"), ("y", "core"))
    return jax.shard_map(
        shards,
        mesh=fine,
        in_specs=(row,) * 5 + (weight,) * 3,
        out_specs=(row,) * 2 + (weight,) * 3,
        check_vma=False,
    )
```

```python
import functools
import math

import jax
import jax.numpy as jnp
from jax import lax
from jax.experimental import pallas as pl
from jax.experimental.pallas import tpu as pltpu
from jax.sharding import Mesh, PartitionSpec as P

SLOTS = 5
BF = jnp.bfloat16
F32 = jnp.float32
ACROSS = ((0,), (0,))
LANES = ((1,), (1,))


def dot(a, b, dims=((1,), (0,))):
    return lax.dot_general(a, b, (dims, ((), ())), preferred_element_type=F32)


def iota(shape, axis):
    return lax.broadcasted_iota(jnp.int32, shape, axis)


def params(size=24):
    return pltpu.CompilerParams(vmem_limit_bytes=size * 1024 * 1024)


def vmem(count):
    return [pl.BlockSpec(memory_space=pltpu.VMEM)] * count


def places(routes_row, experts):
    tokens = routes_row.shape[1]
    picked = iota((experts, tokens), 0) == routes_row
    hot = jnp.where(picked, 1.0, 0.0).astype(BF)
    earlier = jnp.where(iota((tokens, tokens), 0) < iota((tokens, tokens), 1), 1.0, 0.0).astype(BF)
    before = dot(hot, earlier)
    rank = jnp.sum(jnp.where(picked, before, 0.0), axis=0, keepdims=True).astype(jnp.int32)
    return routes_row, rank


def main_rows(expert, rank, half):
    return jnp.where(rank < SLOTS - 1, expert * 8 + half * 4 + rank, -1)


def last_rows(expert, rank, piece):
    return jnp.where(rank == SLOTS - 1, expert * 8 + piece, -1)


def one_hot(rows, target):
    return iota((rows, target.shape[1]), 0) == target


def pack_tokens(scaled, *refs):
    if scaled:
        routes_ref, gates_ref, mask_ref, src, dst = refs
        value = jnp.where(mask_ref[...] == 1, gates_ref[...].astype(F32), 0.0)
    else:
        routes_ref, src, dst = refs
        value = 1.0
    width = src.shape[1]
    rows = dst.shape[0]
    half, piece = width // 2, width // 8
    expert, rank = places(routes_ref[...], rows // 8)

    def spread(target):
        return jnp.where(one_hot(rows, target), value, 0.0).astype(BF)

    main = dot(spread(main_rows(expert, rank, 0)), src[:, :half])
    main += dot(spread(main_rows(expert, rank, 1)), src[:, half:])
    dst[:, :half] = main.astype(BF)
    last = jnp.zeros((rows, piece), F32)
    for k in range(8):
        last += dot(spread(last_rows(expert, rank, k)), src[:, k * piece : (k + 1) * piece])
    dst[:, half:] = last.astype(BF)


def unpack_tokens(routes_ref, gates_ref, r_ref, out_ref, gate_ref):
    width = out_ref.shape[1]
    rows = r_ref.shape[0]
    half, piece = width // 2, width // 8
    expert, rank = places(routes_ref[...], rows // 8)

    def spread(target):
        return jnp.where(one_hot(rows, target), 1.0, 0.0).astype(BF)

    mains = [dot(spread(main_rows(expert, rank, h)), r_ref[:, :half], ACROSS) for h in (0, 1)]
    for k in range(8):
        last = dot(spread(last_rows(expert, rank, k)), r_ref[:, half : half + piece], ACROSS)
        at = (k % 4) * piece
        out_ref[:, k * piece : (k + 1) * piece] = (mains[k // 4][:, at : at + piece] + last).astype(BF)
    lanes = r_ref[:, half + piece :]
    summed = dot(lanes, spread(expert * 8 + rank), ACROSS)
    gate_ref[...] = summed[0:1, :] / gates_ref[...].astype(F32)


def main_order(rows):
    at = iota((rows, rows), 1)
    inner = at % (rows // 2)
    return iota((rows, rows), 0) == (inner // 4) * 8 + (at // (rows // 2)) * 4 + inner % 4


def last_order(rows):
    at = iota((rows, rows), 1)
    return iota((rows, rows), 0) == (at % (rows // 8)) * 8 + at // (rows // 8)


def orders(rows):
    order = jnp.where(main_order(rows), 1.0, 0.0).astype(BF)
    return order, jnp.where(last_order(rows), 1.0, 0.0).astype(BF)


def open_chunks(packed, dst, at, order, order_last):
    rows = packed.shape[0]
    width = dst.shape[1]
    half, piece = width // 2, width // 8
    four, lone = rows // 2, rows // 8
    main = dot(order, packed[:, :half], ACROSS).astype(BF)
    last = dot(order_last, packed[:, half:], ACROSS).astype(BF)
    dst[at : at + four, :half] = main[:four]
    dst[at : at + four, half:] = main[four:]
    for k in range(8):
        dst[at + four : at + four + lone, k * piece : (k + 1) * piece] = last[k * lone : (k + 1) * lone]


def close_chunks(part, column, out, order, order_last):
    rows = out.shape[0]
    width = part.shape[1]
    half, piece = width // 2, width // 8
    four, lone = rows // 2, rows // 8
    stacked = jnp.concatenate([part[:four, :half], part[:four, half:]], axis=0)
    out[:, :half] = dot(order, stacked).astype(BF)
    stacked = jnp.concatenate([part[four:, k * piece : (k + 1) * piece] for k in range(8)], axis=0)
    out[:, half : half + piece] = dot(order_last, stacked).astype(BF)
    column = jnp.broadcast_to(column.astype(BF), (four + lone, 128))
    main = dot(order[:, :four], column[:four])
    pick = iota((rows, lone), 0) == iota((rows, lone), 1) * 8 + 4
    main += dot(jnp.where(pick, 1.0, 0.0).astype(BF), column[four:])
    out[:, half + piece :] = main.astype(BF)


def held_rows(refs):
    return refs[0][...] if len(refs) == 1 else jnp.concatenate([ref[...] for ref in refs], axis=0)


def x_part(counts, *refs):
    refs = list(refs)
    xs = [[refs.pop(0) for _ in range(count)] for count in counts]
    wgu, x_ref, hid_ref, slope_ref, silu_ref, pre = refs
    order, order_last = orders(xs[0][0].shape[0])
    total, both = hid_ref.shape
    block = total // 4
    for b in range(4):
        open_chunks(held_rows(xs[b]), x_ref, b * block, order, order_last)
    pre[...] = dot(x_ref[...], wgu[...], LANES)
    step = math.gcd(block, 32)
    for r in range(0, total, step):
        at = slice(r, r + step)
        gate, up = pre[at, :both], pre[at, both:]
        sig = jax.nn.sigmoid(gate)
        silu = gate * sig
        hid_ref[at, :] = (silu * up).astype(BF)
        slope_ref[at, :] = up * sig * (1.0 + gate * (1.0 - sig))
        silu_ref[at, :] = silu


def call_x_part(xs, wgu):
    rows = xs[0][0].shape[0]
    pairs, width = wgu.shape
    flat = [v for held in xs for v in held]
    total = 4 * (rows // 2 + rows // 8)
    half_units = jax.ShapeDtypeStruct((total, pairs // 2), F32)
    return pl.pallas_call(
        functools.partial(x_part, [len(held) for held in xs]),
        out_shape=[
            jax.ShapeDtypeStruct((total, width), BF),
            jax.ShapeDtypeStruct((total, pairs // 2), BF),
            half_units,
            half_units,
        ],
        in_specs=vmem(len(flat) + 1),
        out_specs=vmem(4),
        scratch_shapes=[pltpu.VMEM((total, pairs), F32)],
        compiler_params=params(),
        cost_estimate=pl.CostEstimate(flops=1000, bytes_accessed=1000, transcendentals=0),
    )(*flat, wgu)


def dy_part(first, counts, *refs):
    refs = list(refs)
    blocks = len(counts)
    dys = [[refs.pop(0) for _ in range(count)] for count in counts]
    hid, slope, silu, wgu, wd = refs[:5]
    outs = refs[5 : 5 + blocks]
    dy_ref, d_ref, back = refs[5 + blocks :]
    total = dy_ref.shape[0]
    both = wd.shape[0]
    block = total // blocks
    begin = first * block
    order, order_last = orders(outs[0].shape[0])
    for b in range(blocks):
        open_chunks(held_rows(dys[b]), dy_ref, b * block, order, order_last)
    back[...] = dot(dy_ref[...], wd[...], LANES)
    step = math.gcd(block, 32)
    columns = []
    for r in range(0, total, step):
        at = slice(r, r + step)
        there = slice(begin + r, begin + r + step)
        bp = back[at, :]
        d_ref[at, :both] = (bp * slope[there, :]).astype(BF)
        d_ref[at, both:] = (bp * silu[there, :]).astype(BF)
        columns.append(jnp.sum(hid[there, :].astype(F32) * bp, axis=1, keepdims=True))
    for b in range(blocks):
        at = b * block
        part = dot(d_ref[at : at + block, :], wgu[...]).astype(BF)
        column = jnp.concatenate(columns[at // step : (at + block) // step], axis=0)
        close_chunks(part, column, outs[b], order, order_last)


def call_dy_part(first, dys, hid, slope, silu, wgu, wd):
    blocks = len(dys)
    packed = dys[0][0].shape[1]
    flat = [v for held in dys for v in held]
    both, width = wd.shape
    total = hid.shape[0] // 4 * blocks
    rows = hid.shape[0] // 4 * 8 // 5
    return pl.pallas_call(
        functools.partial(dy_part, first, [len(held) for held in dys]),
        out_shape=[jax.ShapeDtypeStruct((rows, packed + 128), BF)] * blocks
        + [jax.ShapeDtypeStruct((total, width), BF), jax.ShapeDtypeStruct((total, 2 * both), BF)],
        in_specs=vmem(len(flat) + 5),
        out_specs=vmem(blocks + 2),
        scratch_shapes=[pltpu.VMEM((total, both), F32)],
        compiler_params=params(),
        cost_estimate=pl.CostEstimate(flops=1000, bytes_accessed=1000, transcendentals=0),
    )(*flat, hid, slope, silu, wgu, wd)


def grad_block(own, has_more, units, hid, d1, d2, x, dy1, dy2, *refs):
    out = refs[-1]
    cut = d1.shape[0]
    both = 2 * units
    first = 0 if own else units
    down = dot(hid[:cut], dy1[...], ACROSS) + dot(hid[cut:], dy2[...], ACROSS)
    pair = dot(d1[...], x[:cut], ACROSS) + dot(d2[...], x[cut:], ACROSS)
    values = (pair[first : first + units], pair[both + first : both + first + units], down[first : first + units])
    for i, value in enumerate(values):
        if has_more:
            refs[1 + i][...] = (value + refs[0][i * units : (i + 1) * units].astype(F32)).astype(BF)
        else:
            out[i * units : (i + 1) * units] = value.astype(BF)


def call_grads(own, hid, d1, d2, x, dy1, dy2, more):
    total, width = x.shape
    units = hid.shape[1] // 2
    cols = 512
    full = lambda a: pl.BlockSpec(a.shape, lambda j: (0, 0))
    piece = lambda rows: pl.BlockSpec((rows, cols), lambda j: (0, j))
    if more:
        out_shape, out_specs = [jax.ShapeDtypeStruct((units, width), BF)] * 3, [piece(units)] * 3
    else:
        out_shape, out_specs = [jax.ShapeDtypeStruct((3 * units, width), BF)], [piece(3 * units)]
    return pl.pallas_call(
        functools.partial(grad_block, own, bool(more), units),
        grid=(width // cols,),
        out_shape=out_shape,
        in_specs=[full(hid), full(d1), full(d2), piece(total), piece(dy1.shape[0]), piece(dy2.shape[0])]
        + [piece(3 * units)] * len(more),
        out_specs=out_specs,
        compiler_params=params(),
        cost_estimate=pl.CostEstimate(flops=1000, bytes_accessed=1000, transcendentals=0),
    )(hid, d1, d2, x, dy1, dy2, *more)


def along(v, axis, size, by):
    return lax.ppermute(v, axis, [(i, (i + by) % size) for i in range(size)])


def shards(tokens, cotangent, routes, gates, loss_mask, w_gate, w_up, w_down):
    experts = lax.axis_size("z") * lax.axis_size("x")
    ring = lax.axis_size("y")
    count, width = tokens.shape
    packed = width // 2 + width // 8
    rows = experts * 8
    routes_row = routes.reshape(1, count)
    gates_row = gates.reshape(1, count)
    mask_row = loss_mask.reshape(1, count)

    def pack(*operands):
        return pl.pallas_call(
            functools.partial(pack_tokens, len(operands) > 2),
            out_shape=jax.ShapeDtypeStruct((rows, packed), BF),
            in_specs=vmem(len(operands)),
            out_specs=vmem(1)[0],
            compiler_params=params(56),
        )(*operands)

    def dispatch(v):
        chunks = v.reshape(experts, 8, v.shape[1])
        return lax.all_to_all(chunks, ("z", "x"), 0, 0, tiled=True).reshape(v.shape)

    step = lambda v, by: along(v, "y", ring, by)
    units = w_gate.shape[1]
    flip = lambda v: along(v, "core", 2, 1)
    packed_dy = pack(routes_row, gates_row, mask_row, cotangent)
    packed_dy, *mine = lax.optimization_barrier((packed_dy, w_gate[0], w_up[0], w_down[0]))
    swapped = flip(jnp.concatenate(mine, axis=0))
    theirs = [swapped[i * units : (i + 1) * units] for i in range(3)]
    wgu = jnp.concatenate([mine[0], theirs[0], mine[1], theirs[1]], axis=0)
    wd = jnp.concatenate([mine[2], theirs[2]], axis=0)
    x_own = dispatch(pack(routes_row, tokens))
    x_own, packed_dy = lax.optimization_barrier((x_own, packed_dy))
    dy_own = dispatch(packed_dy)
    cut = rows // 2

    def near(own):
        first, second = own[:cut], own[cut:]
        return step(first, 1), step(second, -1), step(second, 1), step(first, -1)

    def gathered(own, low_first, high_second, low_second, high_first):
        far = [step(low_first, 1), step(high_second, -1)]
        return [[own], [low_first, low_second], [high_first, high_second], far]

    xs = gathered(x_own, *near(x_own))
    x_all, hid, slope, silu = call_x_part(xs, wgu)
    low_first, high_second, low_second, high_first = near(dy_own)
    low_first, high_second, hid = lax.optimization_barrier((low_first, high_second, hid))
    dys = gathered(dy_own, low_first, high_second, low_second, high_first)
    p_own, p_low, p_high, dy1, d1 = call_dy_part(0, dys[:3], hid, slope, silu, wgu, wd)
    p_far, dy2, d2 = call_dy_part(3, dys[3:], hid, slope, silu, wgu, wd)
    arrived = [step(p_low, -1), step(p_high, 1), step(p_far, 2)]
    (given,) = call_grads(False, hid, d1, d2, x_all, dy1, dy2, [])
    *arrived, given = lax.optimization_barrier((*arrived, given))
    taken = flip(given)
    home = p_own.astype(F32)
    for part in arrived:
        home = home + part.astype(F32)
    returned = dispatch(home.astype(BF))
    grads = call_grads(True, hid, d1, d2, x_all, dy1, dy2, [taken])
    returned, *grads = lax.optimization_barrier((returned, *grads))
    grad_tokens, grad_gates = pl.pallas_call(
        unpack_tokens,
        out_shape=[jax.ShapeDtypeStruct((count, width), BF), jax.ShapeDtypeStruct((1, count), F32)],
        in_specs=vmem(3),
        out_specs=vmem(2),
        compiler_params=params(),
    )(routes_row, gates_row, returned)
    return (grad_tokens, grad_gates.reshape(count, 1), *[g[None] for g in grads])


def solution(mesh):
    devices = mesh.devices
    fine = Mesh(devices.reshape(devices.shape[0] // 2, 2, -1, 4), ("y", "core", "z", "x"))
    row = P(("y", "core", "z", "x"))
    weight = P(("z", "x"), ("y", "core"))
    return jax.shard_map(
        shards,
        mesh=fine,
        in_specs=(row,) * 5 + (weight,) * 3,
        out_specs=(row,) * 2 + (weight,) * 3,
        check_vma=False,
    )
```

```python
import functools
import math

import jax
import jax.numpy as jnp
from jax import lax
from jax.experimental import pallas as pl
from jax.experimental.pallas import tpu as pltpu
from jax.sharding import Mesh, PartitionSpec as P

SLOTS = 5
BF = jnp.bfloat16
F32 = jnp.float32
ACROSS = ((0,), (0,))
LANES = ((1,), (1,))


def dot(a, b, dims=((1,), (0,))):
    return lax.dot_general(a, b, (dims, ((), ())), preferred_element_type=F32)


def iota(shape, axis):
    return lax.broadcasted_iota(jnp.int32, shape, axis)


def params(size=24):
    return pltpu.CompilerParams(vmem_limit_bytes=size * 1024 * 1024)


def vmem(count):
    return [pl.BlockSpec(memory_space=pltpu.VMEM)] * count


def places(routes_row, experts):
    tokens = routes_row.shape[1]
    picked = iota((experts, tokens), 0) == routes_row
    hot = jnp.where(picked, 1.0, 0.0).astype(BF)
    earlier = jnp.where(iota((tokens, tokens), 0) < iota((tokens, tokens), 1), 1.0, 0.0).astype(BF)
    before = dot(hot, earlier)
    rank = jnp.sum(jnp.where(picked, before, 0.0), axis=0, keepdims=True).astype(jnp.int32)
    return routes_row, rank


def main_rows(expert, rank, half):
    return jnp.where(rank < SLOTS - 1, expert * 8 + half * 4 + rank, -1)


def last_rows(expert, rank, piece):
    return jnp.where(rank == SLOTS - 1, expert * 8 + piece, -1)


def one_hot(rows, target):
    return iota((rows, target.shape[1]), 0) == target


def pack_tokens(scaled, *refs):
    if scaled:
        routes_ref, gates_ref, mask_ref, src, dst = refs
        value = jnp.where(mask_ref[...] == 1, gates_ref[...].astype(F32), 0.0)
    else:
        routes_ref, src, dst = refs
        value = 1.0
    width = src.shape[1]
    rows = dst.shape[0]
    half, piece = width // 2, width // 8
    expert, rank = places(routes_ref[...], rows // 8)

    def spread(target):
        return jnp.where(one_hot(rows, target), value, 0.0).astype(BF)

    main = dot(spread(main_rows(expert, rank, 0)), src[:, :half])
    main += dot(spread(main_rows(expert, rank, 1)), src[:, half:])
    dst[:, :half] = main.astype(BF)
    last = jnp.zeros((rows, piece), F32)
    for k in range(8):
        last += dot(spread(last_rows(expert, rank, k)), src[:, k * piece : (k + 1) * piece])
    dst[:, half:] = last.astype(BF)


def unpack_tokens(routes_ref, gates_ref, r_ref, out_ref, gate_ref):
    width = out_ref.shape[1]
    rows = r_ref.shape[0]
    half, piece = width // 2, width // 8
    expert, rank = places(routes_ref[...], rows // 8)

    def spread(target):
        return jnp.where(one_hot(rows, target), 1.0, 0.0).astype(BF)

    mains = [dot(spread(main_rows(expert, rank, h)), r_ref[:, :half], ACROSS) for h in (0, 1)]
    for k in range(8):
        last = dot(spread(last_rows(expert, rank, k)), r_ref[:, half : half + piece], ACROSS)
        at = (k % 4) * piece
        out_ref[:, k * piece : (k + 1) * piece] = (mains[k // 4][:, at : at + piece] + last).astype(BF)
    lanes = r_ref[:, half + piece :]
    summed = dot(lanes, spread(expert * 8 + rank), ACROSS)
    gate_ref[...] = summed[0:1, :] / gates_ref[...].astype(F32)


def main_order(rows):
    at = iota((rows, rows), 1)
    inner = at % (rows // 2)
    return iota((rows, rows), 0) == (inner // 4) * 8 + (at // (rows // 2)) * 4 + inner % 4


def last_order(rows):
    at = iota((rows, rows), 1)
    return iota((rows, rows), 0) == (at % (rows // 8)) * 8 + at // (rows // 8)


def orders(rows):
    order = jnp.where(main_order(rows), 1.0, 0.0).astype(BF)
    return order, jnp.where(last_order(rows), 1.0, 0.0).astype(BF)


def open_chunks(packed, dst, at, order, order_last):
    rows = packed.shape[0]
    width = dst.shape[1]
    half, piece = width // 2, width // 8
    four, lone = rows // 2, rows // 8
    main = dot(order, packed[:, :half], ACROSS).astype(BF)
    last = dot(order_last, packed[:, half:], ACROSS).astype(BF)
    dst[at : at + four, :half] = main[:four]
    dst[at : at + four, half:] = main[four:]
    for k in range(8):
        dst[at + four : at + four + lone, k * piece : (k + 1) * piece] = last[k * lone : (k + 1) * lone]


def close_chunks(part, column, outs, order, order_last):
    rows = order.shape[0]
    width = part.shape[1]
    half, piece = width // 2, width // 8
    four, lone = rows // 2, rows // 8
    stacked = jnp.concatenate([part[:four, :half], part[:four, half:]], axis=0)
    packed = [dot(order, stacked).astype(BF)]
    stacked = jnp.concatenate([part[four:, k * piece : (k + 1) * piece] for k in range(8)], axis=0)
    packed.append(dot(order_last, stacked).astype(BF))
    column = jnp.broadcast_to(column.astype(BF), (four + lone, 128))
    main = dot(order[:, :four], column[:four])
    pick = iota((rows, lone), 0) == iota((rows, lone), 1) * 8 + 4
    main += dot(jnp.where(pick, 1.0, 0.0).astype(BF), column[four:])
    packed = jnp.concatenate([*packed, main.astype(BF)], axis=1)
    height = rows // len(outs)
    for i, out in enumerate(outs):
        out[...] = packed[i * height : (i + 1) * height]


def held_rows(refs):
    return refs[0][...] if len(refs) == 1 else jnp.concatenate([ref[...] for ref in refs], axis=0)


def x_part(counts, *refs):
    refs = list(refs)
    xs = [[refs.pop(0) for _ in range(count)] for count in counts]
    wgu, x_ref, hid_ref, slope_ref, silu_ref, pre = refs
    order, order_last = orders(sum(ref.shape[0] for ref in xs[0]))
    total, both = hid_ref.shape
    block = total // len(counts)
    for b in range(len(counts)):
        open_chunks(held_rows(xs[b]), x_ref, b * block, order, order_last)
    pre[...] = dot(x_ref[...], wgu[...], LANES)
    step = math.gcd(block, 32)
    for r in range(0, total, step):
        at = slice(r, r + step)
        gate, up = pre[at, :both], pre[at, both:]
        sig = jax.nn.sigmoid(gate)
        silu = gate * sig
        hid_ref[at, :] = (silu * up).astype(BF)
        slope_ref[at, :] = up * sig * (1.0 + gate * (1.0 - sig))
        silu_ref[at, :] = silu


def call_x_part(xs, wgu):
    rows = sum(v.shape[0] for v in xs[0])
    pairs, width = wgu.shape
    flat = [v for held in xs for v in held]
    total = len(xs) * (rows // 2 + rows // 8)
    half_units = jax.ShapeDtypeStruct((total, pairs // 2), F32)
    return pl.pallas_call(
        functools.partial(x_part, [len(held) for held in xs]),
        out_shape=[
            jax.ShapeDtypeStruct((total, width), BF),
            jax.ShapeDtypeStruct((total, pairs // 2), BF),
            half_units,
            half_units,
        ],
        in_specs=vmem(len(flat) + 1),
        out_specs=vmem(4),
        scratch_shapes=[pltpu.VMEM((total, pairs), F32)],
        compiler_params=params(),
        cost_estimate=pl.CostEstimate(flops=1000, bytes_accessed=1000, transcendentals=0),
    )(*flat, wgu)


def dy_part(counts, *refs):
    refs = list(refs)
    blocks = len(counts)
    dys = [[refs.pop(0) for _ in range(count)] for count in counts]
    hid, slope, silu, wgu, wd = refs[:5]
    dy_ref, d_ref, back = refs[-3:]
    outs = [refs[5 + 2 * b : 7 + 2 * b] for b in range(blocks)]
    total = dy_ref.shape[0]
    both = wd.shape[0]
    block = total // blocks
    order, order_last = orders(2 * outs[0][0].shape[0])
    for b in range(blocks):
        open_chunks(held_rows(dys[b]), dy_ref, b * block, order, order_last)
    back[...] = dot(dy_ref[...], wd[...], LANES)
    step = math.gcd(block, 32)
    columns = []
    for r in range(0, total, step):
        at = slice(r, r + step)
        bp = back[at, :]
        d_ref[at, :both] = (bp * slope[at, :]).astype(BF)
        d_ref[at, both:] = (bp * silu[at, :]).astype(BF)
        columns.append(jnp.sum(hid[at, :].astype(F32) * bp, axis=1, keepdims=True))
    for b in range(blocks):
        at = b * block
        part = dot(d_ref[at : at + block, :], wgu[...]).astype(BF)
        column = jnp.concatenate(columns[at // step : (at + block) // step], axis=0)
        close_chunks(part, column, outs[b], order, order_last)


def call_dy_part(dys, hid, slope, silu, wgu, wd):
    blocks = len(dys)
    packed = dys[0][0].shape[1]
    flat = [v for held in dys for v in held]
    both, width = wd.shape
    total = hid.shape[0]
    rows = total // blocks * 8 // 5
    return pl.pallas_call(
        functools.partial(dy_part, [len(held) for held in dys]),
        out_shape=[jax.ShapeDtypeStruct((rows // 2, packed + 128), BF)] * (2 * blocks)
        + [jax.ShapeDtypeStruct((total, width), BF), jax.ShapeDtypeStruct((total, 2 * both), BF)],
        in_specs=vmem(len(flat) + 5),
        out_specs=vmem(2 * blocks + 2),
        scratch_shapes=[pltpu.VMEM((total, both), F32)],
        compiler_params=params(),
        cost_estimate=pl.CostEstimate(flops=1000, bytes_accessed=1000, transcendentals=0),
    )(*flat, hid, slope, silu, wgu, wd)


def grad_block(own, has_more, units, hid1, hid2, d1, d2, x1, x2, dy1, dy2, *refs):
    out = refs[-1]
    both = 2 * units
    first = 0 if own else units
    down = dot(hid1[...], dy1[...], ACROSS) + dot(hid2[...], dy2[...], ACROSS)
    pair = dot(d1[...], x1[...], ACROSS) + dot(d2[...], x2[...], ACROSS)
    values = (pair[first : first + units], pair[both + first : both + first + units], down[first : first + units])
    for i, value in enumerate(values):
        if has_more:
            refs[1 + i][...] = (value + refs[0][i * units : (i + 1) * units].astype(F32)).astype(BF)
        else:
            out[i * units : (i + 1) * units] = value.astype(BF)


def call_grads(own, acts, rows, more):
    width = rows[0].shape[1]
    units = acts[0].shape[1] // 2
    cols = 512
    full = lambda a: pl.BlockSpec(a.shape, lambda j: (0, 0))
    piece = lambda rows: pl.BlockSpec((rows, cols), lambda j: (0, j))
    if more:
        out_shape, out_specs = [jax.ShapeDtypeStruct((units, width), BF)] * 3, [piece(units)] * 3
    else:
        out_shape, out_specs = [jax.ShapeDtypeStruct((3 * units, width), BF)], [piece(3 * units)]
    return pl.pallas_call(
        functools.partial(grad_block, own, bool(more), units),
        grid=(width // cols,),
        out_shape=out_shape,
        in_specs=[full(a) for a in acts]
        + [piece(r.shape[0]) for r in rows]
        + [piece(3 * units)] * len(more),
        out_specs=out_specs,
        compiler_params=params(52 if more else 14),
        cost_estimate=pl.CostEstimate(flops=1000, bytes_accessed=1000, transcendentals=0),
    )(*acts, *rows, *more)


def add(*parts):
    return sum(part.astype(F32) for part in parts).astype(BF)


def along(v, axis, size, by):
    return lax.ppermute(v, axis, [(i, (i + by) % size) for i in range(size)])


def shards(tokens, cotangent, routes, gates, loss_mask, w_gate, w_up, w_down):
    experts = lax.axis_size("z") * lax.axis_size("x")
    ring = lax.axis_size("y")
    count, width = tokens.shape
    packed = width // 2 + width // 8
    rows = experts * 8
    routes_row = routes.reshape(1, count)
    gates_row = gates.reshape(1, count)
    mask_row = loss_mask.reshape(1, count)

    def pack(*operands):
        return pl.pallas_call(
            functools.partial(pack_tokens, len(operands) > 2),
            out_shape=jax.ShapeDtypeStruct((rows, packed), BF),
            in_specs=vmem(len(operands)),
            out_specs=vmem(1)[0],
            compiler_params=params(56),
        )(*operands)

    def dispatch(v):
        chunks = v.reshape(experts, 8, v.shape[1])
        return lax.all_to_all(chunks, ("z", "x"), 0, 0, tiled=True).reshape(v.shape)

    step = lambda v, by: along(v, "y", ring, by)
    units = w_gate.shape[1]
    flip = lambda v: along(v, "core", 2, 1)
    packed_dy = pack(routes_row, gates_row, mask_row, cotangent)
    packed_dy, *mine = lax.optimization_barrier((packed_dy, w_gate[0], w_up[0], w_down[0]))
    swapped = flip(jnp.concatenate(mine, axis=0))
    theirs = [swapped[i * units : (i + 1) * units] for i in range(3)]
    wgu = jnp.concatenate([mine[0], theirs[0], mine[1], theirs[1]], axis=0)
    wd = jnp.concatenate([mine[2], theirs[2]], axis=0)
    x_own = dispatch(pack(routes_row, tokens))
    x_own, packed_dy = lax.optimization_barrier((x_own, packed_dy))
    dy_own = dispatch(packed_dy)
    cut = rows // 2

    def halves(own):
        return own[:cut], own[cut:]

    def lead(first, second):
        return step(first, 1), step(second, -1)

    def follow(first, second):
        return step(second, 1), step(first, -1)

    first, second = halves(x_own)
    x_lead, x_follow = lead(first, second), follow(first, second)
    x_near = [[x_own], [x_lead[0], x_follow[0]], [x_follow[1], x_lead[1]]]
    x1, hid1, slope1, silu1 = call_x_part(x_near, wgu)
    first, second = halves(dy_own)
    dy_lead = lead(first, second)
    first, second, hid1, *x_far = lax.optimization_barrier((first, second, hid1, *lead(*x_lead)))
    dy_follow = follow(first, second)
    dy_near = [[dy_own], [dy_lead[0], dy_follow[0]], [dy_follow[1], dy_lead[1]]]
    own1, own2, low1, low2, high1, high2, dy1, d1 = call_dy_part(dy_near, hid1, slope1, silu1, wgu, wd)
    x2, hid2, slope2, silu2 = call_x_part([x_far], wgu)
    *dy_far, low1 = lax.optimization_barrier((*lead(*dy_lead), low1))
    far1, far2, dy2, d2 = call_dy_part([dy_far], hid2, slope2, silu2, wgu, wd)
    acts, kept_rows = [hid1, hid2, d1, d2], [x1, x2, dy1, dy2]
    low1, high2 = step(low1, -1), step(high2, 1)
    low2 = step(add(low2, step(far2, -1)), -1)
    high1 = step(add(high1, step(far1, 1)), 1)
    (given,) = call_grads(False, acts, kept_rows, [])
    low1, low2, high1, high2, given = lax.optimization_barrier((low1, low2, high1, high2, given))
    taken = flip(given)
    returned = dispatch(jnp.concatenate([add(own1, low1, high1), add(own2, low2, high2)], axis=0))
    grads = call_grads(True, acts, kept_rows, [taken])
    returned, *grads = lax.optimization_barrier((returned, *grads))
    grad_tokens, grad_gates = pl.pallas_call(
        unpack_tokens,
        out_shape=[jax.ShapeDtypeStruct((count, width), BF), jax.ShapeDtypeStruct((1, count), F32)],
        in_specs=vmem(3),
        out_specs=vmem(2),
        compiler_params=params(),
    )(routes_row, gates_row, returned)
    return (grad_tokens, grad_gates.reshape(count, 1), *[g[None] for g in grads])


def solution(mesh):
    devices = mesh.devices
    fine = Mesh(devices.reshape(devices.shape[0] // 2, 2, -1, 4), ("y", "core", "z", "x"))
    row = P(("y", "core", "z", "x"))
    weight = P(("z", "x"), ("y", "core"))
    return jax.shard_map(
        shards,
        mesh=fine,
        in_specs=(row,) * 5 + (weight,) * 3,
        out_specs=(row,) * 2 + (weight,) * 3,
        check_vma=False,
    )
```

```python
import functools
import math

import jax
import jax.numpy as jnp
from jax import lax
from jax.experimental import pallas as pl
from jax.experimental.pallas import tpu as pltpu
from jax.sharding import Mesh, PartitionSpec as P

SLOTS = 5
BF = jnp.bfloat16
F32 = jnp.float32
ACROSS = ((0,), (0,))
LANES = ((1,), (1,))


def dot(a, b, dims=((1,), (0,))):
    return lax.dot_general(a, b, (dims, ((), ())), preferred_element_type=F32)


def iota(shape, axis):
    return lax.broadcasted_iota(jnp.int32, shape, axis)


def params(size=24):
    return pltpu.CompilerParams(vmem_limit_bytes=size * 1024 * 1024)


def vmem(count):
    return [pl.BlockSpec(memory_space=pltpu.VMEM)] * count


def places(routes_row, experts):
    tokens = routes_row.shape[1]
    picked = iota((experts, tokens), 0) == routes_row
    hot = jnp.where(picked, 1.0, 0.0).astype(BF)
    earlier = jnp.where(iota((tokens, tokens), 0) < iota((tokens, tokens), 1), 1.0, 0.0).astype(BF)
    before = dot(hot, earlier)
    rank = jnp.sum(jnp.where(picked, before, 0.0), axis=0, keepdims=True).astype(jnp.int32)
    return routes_row, rank


def main_rows(expert, rank, half):
    return jnp.where(rank < SLOTS - 1, expert * 8 + half * 4 + rank, -1)


def last_rows(expert, rank, piece):
    return jnp.where(rank == SLOTS - 1, expert * 8 + piece, -1)


def one_hot(rows, target):
    return iota((rows, target.shape[1]), 0) == target


def pack_tokens(scaled, *refs):
    if scaled:
        routes_ref, gates_ref, mask_ref, src, dst = refs
        value = jnp.where(mask_ref[...] == 1, gates_ref[...].astype(F32), 0.0)
    else:
        routes_ref, src, dst = refs
        value = 1.0
    width = src.shape[1]
    rows = dst.shape[0]
    half, piece = width // 2, width // 8
    expert, rank = places(routes_ref[...], rows // 8)

    def spread(target):
        return jnp.where(one_hot(rows, target), value, 0.0).astype(BF)

    hot = jnp.concatenate([spread(main_rows(expert, rank, h)) for h in (0, 1)], axis=1)
    stacked = jnp.concatenate([src[:, :half], src[:, half:]], axis=0)
    dst[:, :half] = dot(hot, stacked).astype(BF)
    hot = jnp.concatenate([spread(last_rows(expert, rank, k)) for k in range(8)], axis=1)
    stacked = jnp.concatenate([src[:, k * piece : (k + 1) * piece] for k in range(8)], axis=0)
    dst[:, half:] = dot(hot, stacked).astype(BF)


def unpack_tokens(routes_ref, gates_ref, r_ref, out_ref, gate_ref):
    width = out_ref.shape[1]
    rows = r_ref.shape[0]
    half, piece = width // 2, width // 8
    expert, rank = places(routes_ref[...], rows // 8)

    def spread(target):
        return jnp.where(one_hot(rows, target), 1.0, 0.0).astype(BF)

    count = out_ref.shape[0]
    hot = jnp.concatenate([spread(main_rows(expert, rank, h)) for h in (0, 1)], axis=1)
    mains = dot(hot, r_ref[:, :half], ACROSS)
    hot = jnp.concatenate([spread(last_rows(expert, rank, k)) for k in range(8)], axis=1)
    lasts = dot(hot, r_ref[:, half : half + piece], ACROSS)
    for k in range(8):
        at = (k % 4) * piece
        main = mains[k // 4 * count : (k // 4 + 1) * count, at : at + piece]
        last = lasts[k * count : (k + 1) * count]
        out_ref[:, k * piece : (k + 1) * piece] = (main + last).astype(BF)
    lanes = r_ref[:, half + piece :]
    summed = dot(lanes, spread(expert * 8 + rank), ACROSS)
    gate_ref[...] = summed[0:1, :] / gates_ref[...].astype(F32)


def main_order(rows):
    at = iota((rows, rows), 1)
    inner = at % (rows // 2)
    return iota((rows, rows), 0) == (inner // 4) * 8 + (at // (rows // 2)) * 4 + inner % 4


def last_order(rows):
    at = iota((rows, rows), 1)
    return iota((rows, rows), 0) == (at % (rows // 8)) * 8 + at // (rows // 8)


def orders(rows):
    order = jnp.where(main_order(rows), 1.0, 0.0).astype(BF)
    return order, jnp.where(last_order(rows), 1.0, 0.0).astype(BF)


def open_chunks(packed, dst, at, order, order_last):
    rows = packed.shape[0]
    width = dst.shape[1]
    half, piece = width // 2, width // 8
    four, lone = rows // 2, rows // 8
    main = dot(order, packed[:, :half], ACROSS).astype(BF)
    last = dot(order_last, packed[:, half:], ACROSS).astype(BF)
    dst[at : at + four, :half] = main[:four]
    dst[at : at + four, half:] = main[four:]
    for k in range(8):
        dst[at + four : at + four + lone, k * piece : (k + 1) * piece] = last[k * lone : (k + 1) * lone]


def close_chunks(part, column, outs, order, order_last):
    rows = order.shape[0]
    width = part.shape[1]
    half, piece = width // 2, width // 8
    four, lone = rows // 2, rows // 8
    stacked = jnp.concatenate([part[:four, :half], part[:four, half:]], axis=0)
    packed = [dot(order, stacked).astype(BF)]
    stacked = jnp.concatenate([part[four:, k * piece : (k + 1) * piece] for k in range(8)], axis=0)
    packed.append(dot(order_last, stacked).astype(BF))
    column = jnp.broadcast_to(column.astype(BF), (four + lone, 128))
    main = dot(order[:, :four], column[:four])
    pick = iota((rows, lone), 0) == iota((rows, lone), 1) * 8 + 4
    main += dot(jnp.where(pick, 1.0, 0.0).astype(BF), column[four:])
    packed = jnp.concatenate([*packed, main.astype(BF)], axis=1)
    height = rows // len(outs)
    for i, out in enumerate(outs):
        out[...] = packed[i * height : (i + 1) * height]


def held_rows(refs):
    return refs[0][...] if len(refs) == 1 else jnp.concatenate([ref[...] for ref in refs], axis=0)


def x_part(counts, *refs):
    refs = list(refs)
    xs = [[refs.pop(0) for _ in range(count)] for count in counts]
    wgu, x_ref, hid_ref, slope_ref, silu_ref, pre = refs
    order, order_last = orders(sum(ref.shape[0] for ref in xs[0]))
    total, both = hid_ref.shape
    block = total // len(counts)
    for b in range(len(counts)):
        open_chunks(held_rows(xs[b]), x_ref, b * block, order, order_last)
    pre[...] = dot(x_ref[...], wgu[...], LANES)
    step = math.gcd(block, 32)
    for r in range(0, total, step):
        at = slice(r, r + step)
        gate, up = pre[at, :both], pre[at, both:]
        sig = jax.nn.sigmoid(gate)
        silu = gate * sig
        hid_ref[at, :] = (silu * up).astype(BF)
        slope_ref[at, :] = up * sig * (1.0 + gate * (1.0 - sig))
        silu_ref[at, :] = silu


def call_x_part(xs, wgu):
    rows = sum(v.shape[0] for v in xs[0])
    pairs, width = wgu.shape
    flat = [v for held in xs for v in held]
    total = len(xs) * (rows // 2 + rows // 8)
    half_units = jax.ShapeDtypeStruct((total, pairs // 2), F32)
    return pl.pallas_call(
        functools.partial(x_part, [len(held) for held in xs]),
        out_shape=[
            jax.ShapeDtypeStruct((total, width), BF),
            jax.ShapeDtypeStruct((total, pairs // 2), BF),
            half_units,
            half_units,
        ],
        in_specs=vmem(len(flat) + 1),
        out_specs=vmem(4),
        scratch_shapes=[pltpu.VMEM((total, pairs), F32)],
        compiler_params=params(),
        cost_estimate=pl.CostEstimate(flops=1000, bytes_accessed=1000, transcendentals=0),
    )(*flat, wgu)


def dy_part(counts, *refs):
    refs = list(refs)
    blocks = len(counts)
    dys = [[refs.pop(0) for _ in range(count)] for count in counts]
    hid, slope, silu, wgu, wd = refs[:5]
    dy_ref, d_ref, back = refs[-3:]
    outs = [refs[5 + 2 * b : 7 + 2 * b] for b in range(blocks)]
    total = dy_ref.shape[0]
    both = wd.shape[0]
    block = total // blocks
    order, order_last = orders(2 * outs[0][0].shape[0])
    for b in range(blocks):
        open_chunks(held_rows(dys[b]), dy_ref, b * block, order, order_last)
    back[...] = dot(dy_ref[...], wd[...], LANES)
    step = math.gcd(block, 32)
    columns = []
    for r in range(0, total, step):
        at = slice(r, r + step)
        bp = back[at, :]
        d_ref[at, :both] = (bp * slope[at, :]).astype(BF)
        d_ref[at, both:] = (bp * silu[at, :]).astype(BF)
        columns.append(jnp.sum(hid[at, :].astype(F32) * bp, axis=1, keepdims=True))
    for b in range(blocks):
        at = b * block
        part = dot(d_ref[at : at + block, :], wgu[...]).astype(BF)
        column = jnp.concatenate(columns[at // step : (at + block) // step], axis=0)
        close_chunks(part, column, outs[b], order, order_last)


def call_dy_part(dys, hid, slope, silu, wgu, wd):
    blocks = len(dys)
    packed = dys[0][0].shape[1]
    flat = [v for held in dys for v in held]
    both, width = wd.shape
    total = hid.shape[0]
    rows = total // blocks * 8 // 5
    return pl.pallas_call(
        functools.partial(dy_part, [len(held) for held in dys]),
        out_shape=[jax.ShapeDtypeStruct((rows // 2, packed + 128), BF)] * (2 * blocks)
        + [jax.ShapeDtypeStruct((total, width), BF), jax.ShapeDtypeStruct((total, 2 * both), BF)],
        in_specs=vmem(len(flat) + 5),
        out_specs=vmem(2 * blocks + 2),
        scratch_shapes=[pltpu.VMEM((total, both), F32)],
        compiler_params=params(),
        cost_estimate=pl.CostEstimate(flops=1000, bytes_accessed=1000, transcendentals=0),
    )(*flat, hid, slope, silu, wgu, wd)


def grad_block(own, has_more, units, hid1, hid2, d1, d2, x1, x2, dy1, dy2, *refs):
    out = refs[-1]
    both = 2 * units
    first = 0 if own else units
    down = dot(hid1[...], dy1[...], ACROSS) + dot(hid2[...], dy2[...], ACROSS)
    pair = dot(d1[...], x1[...], ACROSS) + dot(d2[...], x2[...], ACROSS)
    values = (pair[first : first + units], pair[both + first : both + first + units], down[first : first + units])
    for i, value in enumerate(values):
        if has_more:
            refs[1 + i][...] = (value + refs[0][i * units : (i + 1) * units].astype(F32)).astype(BF)
        else:
            out[i * units : (i + 1) * units] = value.astype(BF)


def call_grads(own, acts, rows, more):
    width = rows[0].shape[1]
    units = acts[0].shape[1] // 2
    cols = 512
    full = lambda a: pl.BlockSpec(a.shape, lambda j: (0, 0))
    piece = lambda rows: pl.BlockSpec((rows, cols), lambda j: (0, j))
    if more:
        out_shape, out_specs = [jax.ShapeDtypeStruct((units, width), BF)] * 3, [piece(units)] * 3
    else:
        out_shape, out_specs = [jax.ShapeDtypeStruct((3 * units, width), BF)], [piece(3 * units)]
    return pl.pallas_call(
        functools.partial(grad_block, own, bool(more), units),
        grid=(width // cols,),
        out_shape=out_shape,
        in_specs=[full(a) for a in acts]
        + [piece(r.shape[0]) for r in rows]
        + [piece(3 * units)] * len(more),
        out_specs=out_specs,
        compiler_params=params(52 if more else 14),
        cost_estimate=pl.CostEstimate(flops=1000, bytes_accessed=1000, transcendentals=0),
    )(*acts, *rows, *more)


def add(*parts):
    return sum(part.astype(F32) for part in parts).astype(BF)


def along(v, axis, size, by):
    return lax.ppermute(v, axis, [(i, (i + by) % size) for i in range(size)])


def shards(tokens, cotangent, routes, gates, loss_mask, w_gate, w_up, w_down):
    experts = lax.axis_size("z") * lax.axis_size("x")
    ring = lax.axis_size("y")
    count, width = tokens.shape
    packed = width // 2 + width // 8
    rows = experts * 8
    routes_row = routes.reshape(1, count)
    gates_row = gates.reshape(1, count)
    mask_row = loss_mask.reshape(1, count)

    def pack(*operands):
        return pl.pallas_call(
            functools.partial(pack_tokens, len(operands) > 2),
            out_shape=jax.ShapeDtypeStruct((rows, packed), BF),
            in_specs=vmem(len(operands)),
            out_specs=vmem(1)[0],
            compiler_params=params(56),
        )(*operands)

    def dispatch(v):
        chunks = v.reshape(experts, 8, v.shape[1])
        return lax.all_to_all(chunks, ("z", "x"), 0, 0, tiled=True).reshape(v.shape)

    step = lambda v, by: along(v, "y", ring, by)
    units = w_gate.shape[1]
    flip = lambda v: along(v, "core", 2, 1)
    packed_dy = pack(routes_row, gates_row, mask_row, cotangent)
    packed_dy, *mine = lax.optimization_barrier((packed_dy, w_gate[0], w_up[0], w_down[0]))
    swapped = flip(jnp.concatenate(mine, axis=0))
    theirs = [swapped[i * units : (i + 1) * units] for i in range(3)]
    wgu = jnp.concatenate([mine[0], theirs[0], mine[1], theirs[1]], axis=0)
    wd = jnp.concatenate([mine[2], theirs[2]], axis=0)
    x_own = dispatch(pack(routes_row, tokens))
    x_own, packed_dy = lax.optimization_barrier((x_own, packed_dy))
    dy_own = dispatch(packed_dy)
    cut = rows // 2

    def halves(own):
        return own[:cut], own[cut:]

    def lead(first, second):
        return step(first, 1), step(second, -1)

    def follow(first, second):
        return step(second, 1), step(first, -1)

    first, second = halves(x_own)
    x_lead, x_follow = lead(first, second), follow(first, second)
    x_near = [[x_own], [x_lead[0], x_follow[0]], [x_follow[1], x_lead[1]]]
    x1, hid1, slope1, silu1 = call_x_part(x_near, wgu)
    first, second = halves(dy_own)
    dy_lead = lead(first, second)
    first, second, hid1, *x_far = lax.optimization_barrier((first, second, hid1, *lead(*x_lead)))
    dy_follow = follow(first, second)
    dy_near = [[dy_own], [dy_lead[0], dy_follow[0]], [dy_follow[1], dy_lead[1]]]
    own1, own2, low1, low2, high1, high2, dy1, d1 = call_dy_part(dy_near, hid1, slope1, silu1, wgu, wd)
    x2, hid2, slope2, silu2 = call_x_part([x_far], wgu)
    *dy_far, low1 = lax.optimization_barrier((*lead(*dy_lead), low1))
    far1, far2, dy2, d2 = call_dy_part([dy_far], hid2, slope2, silu2, wgu, wd)
    acts, kept_rows = [hid1, hid2, d1, d2], [x1, x2, dy1, dy2]
    low1, high2 = step(low1, -1), step(high2, 1)
    low2 = step(add(low2, step(far2, -1)), -1)
    high1 = step(add(high1, step(far1, 1)), 1)
    (given,) = call_grads(False, acts, kept_rows, [])
    low1, low2, high1, high2, given = lax.optimization_barrier((low1, low2, high1, high2, given))
    taken = flip(given)
    returned = dispatch(jnp.concatenate([add(own1, low1, high1), add(own2, low2, high2)], axis=0))
    grads = call_grads(True, acts, kept_rows, [taken])
    returned, *grads = lax.optimization_barrier((returned, *grads))
    grad_tokens, grad_gates = pl.pallas_call(
        unpack_tokens,
        out_shape=[jax.ShapeDtypeStruct((count, width), BF), jax.ShapeDtypeStruct((1, count), F32)],
        in_specs=vmem(3),
        out_specs=vmem(2),
        compiler_params=params(),
    )(routes_row, gates_row, returned)
    return (grad_tokens, grad_gates.reshape(count, 1), *[g[None] for g in grads])


def solution(mesh):
    devices = mesh.devices
    fine = Mesh(devices.reshape(devices.shape[0] // 2, 2, -1, 4), ("y", "core", "z", "x"))
    row = P(("y", "core", "z", "x"))
    weight = P(("z", "x"), ("y", "core"))
    return jax.shard_map(
        shards,
        mesh=fine,
        in_specs=(row,) * 5 + (weight,) * 3,
        out_specs=(row,) * 2 + (weight,) * 3,
        check_vma=False,
    )
```

```python
import functools
import math

import jax
import jax.numpy as jnp
from jax import lax
from jax.experimental import pallas as pl
from jax.experimental.pallas import tpu as pltpu
from jax.sharding import Mesh, PartitionSpec as P

SLOTS = 5
BF = jnp.bfloat16
F32 = jnp.float32
ACROSS = ((0,), (0,))
LANES = ((1,), (1,))


def dot(a, b, dims=((1,), (0,))):
    return lax.dot_general(a, b, (dims, ((), ())), preferred_element_type=F32)


def iota(shape, axis):
    return lax.broadcasted_iota(jnp.int32, shape, axis)


def params(size=24):
    return pltpu.CompilerParams(vmem_limit_bytes=size * 1024 * 1024)


def vmem(count):
    return [pl.BlockSpec(memory_space=pltpu.VMEM)] * count


def places(routes_row, experts):
    tokens = routes_row.shape[1]
    picked = iota((experts, tokens), 0) == routes_row
    hot = jnp.where(picked, 1.0, 0.0).astype(BF)
    earlier = jnp.where(iota((tokens, tokens), 0) < iota((tokens, tokens), 1), 1.0, 0.0).astype(BF)
    before = dot(hot, earlier)
    rank = jnp.sum(jnp.where(picked, before, 0.0), axis=0, keepdims=True).astype(jnp.int32)
    return routes_row, rank


def main_rows(expert, rank, half):
    return jnp.where(rank < SLOTS - 1, expert * 8 + half * 4 + rank, -1)


def last_rows(expert, rank, piece):
    return jnp.where(rank == SLOTS - 1, expert * 8 + piece, -1)


def one_hot(rows, target):
    return iota((rows, target.shape[1]), 0) == target


def pack_tokens(scaled, *refs):
    if scaled:
        routes_ref, gates_ref, mask_ref, src, dst = refs
        value = jnp.where(mask_ref[...] == 1, gates_ref[...].astype(F32), 0.0)
    else:
        routes_ref, src, dst = refs
        value = 1.0
    width = src.shape[1]
    rows = dst.shape[0]
    half, piece = width // 2, width // 8
    expert, rank = places(routes_ref[...], rows // 8)

    def spread(target):
        return jnp.where(one_hot(rows, target), value, 0.0).astype(BF)

    main = dot(spread(main_rows(expert, rank, 0)), src[:, :half])
    main += dot(spread(main_rows(expert, rank, 1)), src[:, half:])
    dst[:, :half] = main.astype(BF)
    last = jnp.zeros((rows, piece), F32)
    for k in range(8):
        last += dot(spread(last_rows(expert, rank, k)), src[:, k * piece : (k + 1) * piece])
    dst[:, half:] = last.astype(BF)


def unpack_tokens(routes_ref, gates_ref, r_ref, out_ref, gate_ref):
    width = out_ref.shape[1]
    rows = r_ref.shape[0]
    half, piece = width // 2, width // 8
    expert, rank = places(routes_ref[...], rows // 8)

    def spread(target):
        return jnp.where(one_hot(rows, target), 1.0, 0.0).astype(BF)

    mains = [dot(spread(main_rows(expert, rank, h)), r_ref[:, :half], ACROSS) for h in (0, 1)]
    for k in range(8):
        last = dot(spread(last_rows(expert, rank, k)), r_ref[:, half : half + piece], ACROSS)
        at = (k % 4) * piece
        out_ref[:, k * piece : (k + 1) * piece] = (mains[k // 4][:, at : at + piece] + last).astype(BF)
    lanes = r_ref[:, half + piece :]
    summed = dot(lanes, spread(expert * 8 + rank), ACROSS)
    gate_ref[...] = summed[0:1, :] / gates_ref[...].astype(F32)


def main_order(rows):
    at = iota((rows, rows), 1)
    inner = at % (rows // 2)
    return iota((rows, rows), 0) == (inner // 4) * 8 + (at // (rows // 2)) * 4 + inner % 4


def last_order(rows):
    at = iota((rows, rows), 1)
    return iota((rows, rows), 0) == (at % (rows // 8)) * 8 + at // (rows // 8)


def orders(rows):
    order = jnp.where(main_order(rows), 1.0, 0.0).astype(BF)
    return order, jnp.where(last_order(rows), 1.0, 0.0).astype(BF)


def open_chunks(packed, dst, at, order, order_last):
    rows = packed.shape[0]
    width = dst.shape[1]
    half, piece = width // 2, width // 8
    four, lone = rows // 2, rows // 8
    main = dot(order, packed[:, :half], ACROSS).astype(BF)
    last = dot(order_last, packed[:, half:], ACROSS).astype(BF)
    dst[at : at + four, :half] = main[:four]
    dst[at : at + four, half:] = main[four:]
    for k in range(8):
        dst[at + four : at + four + lone, k * piece : (k + 1) * piece] = last[k * lone : (k + 1) * lone]


def close_chunks(part, column, outs, order, order_last):
    rows = order.shape[0]
    width = part.shape[1]
    half, piece = width // 2, width // 8
    four, lone = rows // 2, rows // 8
    stacked = jnp.concatenate([part[:four, :half], part[:four, half:]], axis=0)
    packed = [dot(order, stacked).astype(BF)]
    stacked = jnp.concatenate([part[four:, k * piece : (k + 1) * piece] for k in range(8)], axis=0)
    packed.append(dot(order_last, stacked).astype(BF))
    column = jnp.broadcast_to(column.astype(BF), (four + lone, 128))
    main = dot(order[:, :four], column[:four])
    pick = iota((rows, lone), 0) == iota((rows, lone), 1) * 8 + 4
    main += dot(jnp.where(pick, 1.0, 0.0).astype(BF), column[four:])
    packed = jnp.concatenate([*packed, main.astype(BF)], axis=1)
    height = rows // len(outs)
    for i, out in enumerate(outs):
        out[...] = packed[i * height : (i + 1) * height]


def held_rows(refs):
    return refs[0][...] if len(refs) == 1 else jnp.concatenate([ref[...] for ref in refs], axis=0)


def x_part(counts, *refs):
    refs = list(refs)
    xs = [[refs.pop(0) for _ in range(count)] for count in counts]
    wgu, x_ref, hid_ref, slope_ref, silu_ref, pre = refs
    order, order_last = orders(sum(ref.shape[0] for ref in xs[0]))
    total, both = hid_ref.shape
    block = total // len(counts)
    for b in range(len(counts)):
        open_chunks(held_rows(xs[b]), x_ref, b * block, order, order_last)
    pre[...] = dot(x_ref[...], wgu[...], LANES)
    step = math.gcd(block, 32)
    for r in range(0, total, step):
        at = slice(r, r + step)
        gate, up = pre[at, :both], pre[at, both:]
        sig = jax.nn.sigmoid(gate)
        silu = gate * sig
        hid_ref[at, :] = (silu * up).astype(BF)
        slope_ref[at, :] = up * sig * (1.0 + gate * (1.0 - sig))
        silu_ref[at, :] = silu


def call_x_part(xs, wgu):
    rows = sum(v.shape[0] for v in xs[0])
    pairs, width = wgu.shape
    flat = [v for held in xs for v in held]
    total = len(xs) * (rows // 2 + rows // 8)
    half_units = jax.ShapeDtypeStruct((total, pairs // 2), F32)
    return pl.pallas_call(
        functools.partial(x_part, [len(held) for held in xs]),
        out_shape=[
            jax.ShapeDtypeStruct((total, width), BF),
            jax.ShapeDtypeStruct((total, pairs // 2), BF),
            half_units,
            half_units,
        ],
        in_specs=vmem(len(flat) + 1),
        out_specs=vmem(4),
        scratch_shapes=[pltpu.VMEM((total, pairs), F32)],
        compiler_params=params(),
        cost_estimate=pl.CostEstimate(flops=1000, bytes_accessed=1000, transcendentals=0),
    )(*flat, wgu)


def dy_part(counts, *refs):
    refs = list(refs)
    blocks = len(counts)
    dys = [[refs.pop(0) for _ in range(count)] for count in counts]
    hid, slope, silu, wgu, wd = refs[:5]
    dy_ref, d_ref, back = refs[-3:]
    outs = [refs[5 + 2 * b : 7 + 2 * b] for b in range(blocks)]
    total = dy_ref.shape[0]
    both = wd.shape[0]
    block = total // blocks
    order, order_last = orders(2 * outs[0][0].shape[0])
    for b in range(blocks):
        open_chunks(held_rows(dys[b]), dy_ref, b * block, order, order_last)
    back[...] = dot(dy_ref[...], wd[...], LANES)
    step = math.gcd(block, 32)
    columns = []
    for r in range(0, total, step):
        at = slice(r, r + step)
        bp = back[at, :]
        d_ref[at, :both] = (bp * slope[at, :]).astype(BF)
        d_ref[at, both:] = (bp * silu[at, :]).astype(BF)
        columns.append(jnp.sum(hid[at, :].astype(F32) * bp, axis=1, keepdims=True))
    for b in range(blocks):
        at = b * block
        part = dot(d_ref[at : at + block, :], wgu[...]).astype(BF)
        column = jnp.concatenate(columns[at // step : (at + block) // step], axis=0)
        close_chunks(part, column, outs[b], order, order_last)


def call_dy_part(dys, hid, slope, silu, wgu, wd):
    blocks = len(dys)
    packed = dys[0][0].shape[1]
    flat = [v for held in dys for v in held]
    both, width = wd.shape
    total = hid.shape[0]
    rows = total // blocks * 8 // 5
    return pl.pallas_call(
        functools.partial(dy_part, [len(held) for held in dys]),
        out_shape=[jax.ShapeDtypeStruct((rows // 2, packed + 128), BF)] * (2 * blocks)
        + [jax.ShapeDtypeStruct((total, width), BF), jax.ShapeDtypeStruct((total, 2 * both), BF)],
        in_specs=vmem(len(flat) + 5),
        out_specs=vmem(2 * blocks + 2),
        scratch_shapes=[pltpu.VMEM((total, both), F32)],
        compiler_params=params(),
        cost_estimate=pl.CostEstimate(flops=1000, bytes_accessed=1000, transcendentals=0),
    )(*flat, hid, slope, silu, wgu, wd)


def grad_block(own, has_more, units, hid1, hid2, d1, d2, x1, x2, dy1, dy2, *refs):
    out = refs[-1]
    both = 2 * units
    first = 0 if own else units
    down = dot(hid1[...], dy1[...], ACROSS) + dot(hid2[...], dy2[...], ACROSS)
    pair = dot(d1[...], x1[...], ACROSS) + dot(d2[...], x2[...], ACROSS)
    values = (pair[first : first + units], pair[both + first : both + first + units], down[first : first + units])
    for i, value in enumerate(values):
        if has_more:
            refs[1 + i][...] = (value + refs[0][i * units : (i + 1) * units].astype(F32)).astype(BF)
        else:
            out[i * units : (i + 1) * units] = value.astype(BF)


def call_grads(own, acts, rows, more):
    width = rows[0].shape[1]
    units = acts[0].shape[1] // 2
    cols = 512
    full = lambda a: pl.BlockSpec(a.shape, lambda j: (0, 0))
    piece = lambda rows: pl.BlockSpec((rows, cols), lambda j: (0, j))
    if more:
        out_shape, out_specs = [jax.ShapeDtypeStruct((units, width), BF)] * 3, [piece(units)] * 3
    else:
        out_shape, out_specs = [jax.ShapeDtypeStruct((3 * units, width), BF)], [piece(3 * units)]
    return pl.pallas_call(
        functools.partial(grad_block, own, bool(more), units),
        grid=(width // cols,),
        out_shape=out_shape,
        in_specs=[full(a) for a in acts]
        + [piece(r.shape[0]) for r in rows]
        + [piece(3 * units)] * len(more),
        out_specs=out_specs,
        compiler_params=params(52 if more else 14),
        cost_estimate=pl.CostEstimate(flops=1000 if more else 7680 * units * width, bytes_accessed=1000, transcendentals=0),
    )(*acts, *rows, *more)


def add(*parts):
    return sum(part.astype(F32) for part in parts).astype(BF)


def along(v, axis, size, by):
    return lax.ppermute(v, axis, [(i, (i + by) % size) for i in range(size)])


def shards(tokens, cotangent, routes, gates, loss_mask, w_gate, w_up, w_down):
    experts = lax.axis_size("z") * lax.axis_size("x")
    ring = lax.axis_size("y")
    count, width = tokens.shape
    packed = width // 2 + width // 8
    rows = experts * 8
    routes_row = routes.reshape(1, count)
    gates_row = gates.reshape(1, count)
    mask_row = loss_mask.reshape(1, count)

    def pack(*operands):
        return pl.pallas_call(
            functools.partial(pack_tokens, len(operands) > 2),
            out_shape=jax.ShapeDtypeStruct((rows, packed), BF),
            in_specs=vmem(len(operands)),
            out_specs=vmem(1)[0],
            compiler_params=params(56),
        )(*operands)

    def dispatch(v):
        chunks = v.reshape(experts, 8, v.shape[1])
        return lax.all_to_all(chunks, ("z", "x"), 0, 0, tiled=True).reshape(v.shape)

    step = lambda v, by: along(v, "y", ring, by)
    units = w_gate.shape[1]
    flip = lambda v: along(v, "core", 2, 1)
    packed_dy = pack(routes_row, gates_row, mask_row, cotangent)
    packed_dy, *mine = lax.optimization_barrier((packed_dy, w_gate[0], w_up[0], w_down[0]))
    swapped = flip(jnp.concatenate(mine, axis=0))
    theirs = [swapped[i * units : (i + 1) * units] for i in range(3)]
    wgu = jnp.concatenate([mine[0], theirs[0], mine[1], theirs[1]], axis=0)
    wd = jnp.concatenate([mine[2], theirs[2]], axis=0)
    x_own = dispatch(pack(routes_row, tokens))
    x_own, packed_dy = lax.optimization_barrier((x_own, packed_dy))
    dy_own = dispatch(packed_dy)
    cut = rows // 2

    def halves(own):
        return own[:cut], own[cut:]

    def lead(first, second):
        return step(first, 1), step(second, -1)

    def follow(first, second):
        return step(second, 1), step(first, -1)

    first, second = halves(x_own)
    x_lead, x_follow = lead(first, second), follow(first, second)
    x_near = [[x_own], [x_lead[0], x_follow[0]], [x_follow[1], x_lead[1]]]
    x1, hid1, slope1, silu1 = call_x_part(x_near, wgu)
    first, second = halves(dy_own)
    dy_lead = lead(first, second)
    first, second, hid1, *x_far = lax.optimization_barrier((first, second, hid1, *lead(*x_lead)))
    dy_follow = follow(first, second)
    dy_near = [[dy_own], [dy_lead[0], dy_follow[0]], [dy_follow[1], dy_lead[1]]]
    own1, own2, low1, low2, high1, high2, dy1, d1 = call_dy_part(dy_near, hid1, slope1, silu1, wgu, wd)
    x2, hid2, slope2, silu2 = call_x_part([x_far], wgu)
    *dy_far, low1 = lax.optimization_barrier((*lead(*dy_lead), low1))
    far1, far2, dy2, d2 = call_dy_part([dy_far], hid2, slope2, silu2, wgu, wd)
    acts, kept_rows = [hid1, hid2, d1, d2], [x1, x2, dy1, dy2]
    low1, high2 = step(low1, -1), step(high2, 1)
    low2 = step(add(low2, step(far2, -1)), -1)
    high1 = step(add(high1, step(far1, 1)), 1)
    (given,) = call_grads(False, acts, kept_rows, [])
    low1, low2, high1, high2, given = lax.optimization_barrier((low1, low2, high1, high2, given))
    taken = flip(given)
    returned = dispatch(jnp.concatenate([add(own1, low1, high1), add(own2, low2, high2)], axis=0))
    grads = call_grads(True, acts, kept_rows, [taken])
    returned, *grads = lax.optimization_barrier((returned, *grads))
    grad_tokens, grad_gates = pl.pallas_call(
        unpack_tokens,
        out_shape=[jax.ShapeDtypeStruct((count, width), BF), jax.ShapeDtypeStruct((1, count), F32)],
        in_specs=vmem(3),
        out_specs=vmem(2),
        compiler_params=params(),
    )(routes_row, gates_row, returned)
    return (grad_tokens, grad_gates.reshape(count, 1), *[g[None] for g in grads])


def solution(mesh):
    devices = mesh.devices
    fine = Mesh(devices.reshape(devices.shape[0] // 2, 2, -1, 4), ("y", "core", "z", "x"))
    row = P(("y", "core", "z", "x"))
    weight = P(("z", "x"), ("y", "core"))
    return jax.shard_map(
        shards,
        mesh=fine,
        in_specs=(row,) * 5 + (weight,) * 3,
        out_specs=(row,) * 2 + (weight,) * 3,
        check_vma=False,
    )
```
